512 devices in a mesh: ctx: 64 (over y_hi, x, z), tp: 4 (over y_lo), dp: 2 (over core).
Axes of the slice: x: 4, y: 8 (y_hi: 2, y_lo: 4; y = y_hi * 4 + y_lo), z: 8, core: 2. Of those that a mesh axis runs over, the one named last changes fastest.
Arguments:
- gate_query: bfloat16 [2, 8192, 8192], P('dp', 'ctx', 'tp'), may hold values from -6 to 6
- gate_key: bfloat16 [2, 8192, 8192], P('dp', 'ctx', 'tp'), may hold values from -6 to 6
- input_value: bfloat16 [2, 8192, 8192], P('dp', 'ctx', 'tp'), may hold values from -6 to 6
- out_grad: bfloat16 [2, 8192, 8192], P('dp', 'ctx', 'tp'), may hold values from -16 to 16
- short_taps: float32 [7, 8192], P(None, 'tp'), may hold values from -2 to 2
- long_taps: bfloat16 [128, 8192], P(None, 'tp'), may hold values from -0.5 to 0.5
Outputs:
- query_grad: bfloat16 [2, 8192, 8192], P('dp', 'ctx', 'tp')
- key_grad: bfloat16 [2, 8192, 8192], P('dp', 'ctx', 'tp')
- value_grad: bfloat16 [2, 8192, 8192], P('dp', 'ctx', 'tp')
- long_grad: bfloat16 [128, 8192], P(None, 'tp')
- short_grad: bfloat16 [7, 8192], P(None, 'tp')
The draws below stay inside these ranges and needn't reach their ends.
All inputs are finite; a program needn't handle non-finite values.
Results may differ from the reference program's by a relative error of at most 0.013.
Values may be sent and summed in bfloat16 or wider, within the bound.
No kernel may reach another device: no remote copies, remote signals or barrier semaphores. Data moves between devices by JAX's collectives and lax.ppermute only.
A program may use at most 64 MiB of HBM per device.

```python
import math
import jax
import jax.numpy as jnp
from jax import lax

CHANNELS = 8192
KS = 7
KM = 128
LENGTH = 8192
WINDOWS = 2


def draw_out_grad(key, part):
    key = jax.random.fold_in(key, 17)
    primary_key, channel_key = jax.random.split(key, 2)
    extent = (WINDOWS, LENGTH, CHANNELS)
    position = jnp.arange(CHANNELS, dtype=jnp.float32) / CHANNELS
    channel_scale = jnp.exp(jax.random.uniform(channel_key, (CHANNELS,), jnp.float32, 0.0, math.log(5.0)))
    primary = jnp.clip(jax.random.normal(primary_key, extent, jnp.float32), -4.0, 4.0)
    result = primary * channel_scale * (1.0 + 1.2 * position) / 2.5
    return jnp.clip(result, -16.0, 16.0).astype(jnp.bfloat16)


def levels(rng, dims, pieces, smallest, largest):
    gain, own = 1.0, jax.random.fold_in(rng, 6)
    for axis_at, parts in pieces:
        draws = jnp.exp(jax.random.uniform(jax.random.fold_in(own, axis_at), (parts,), jnp.float32, smallest / len(pieces), largest / len(pieces)))
        gain = gain * jnp.repeat(draws, dims[axis_at] // parts).reshape([-1 if axis == axis_at else 1 for axis in range(len(dims))])
    return gain


def normal_values(rng, shape, spread, most, cuts=(), held_as=jnp.bfloat16):
    factor_of = levels(rng, shape, cuts, -0.22, 0.18) if cuts else 1.0
    values = jax.random.normal(rng, shape, jnp.float32) * spread * factor_of
    return jnp.minimum(jnp.maximum(values, -most), most).astype(held_as)


def setup_inputs(seed: int = 0) -> dict:
    key_of = jax.random.split(jax.random.key(seed), 7)
    gate_query = normal_values(key_of[0], (WINDOWS, LENGTH, CHANNELS), 1.0, 6.0, ((0, 2), (1, 64), (2, 4)))
    gate_key = normal_values(key_of[1], (WINDOWS, LENGTH, CHANNELS), 1.0, 6.0, ((0, 2), (1, 64), (2, 4)))
    input_value = normal_values(key_of[2], (WINDOWS, LENGTH, CHANNELS), 1.0, 6.0, ((0, 2), (1, 64), (2, 4)))
    out_grad = draw_out_grad(jax.random.fold_in(key_of[6], 71), 0)
    short_taps = normal_values(key_of[4], (KS, CHANNELS), KS ** -0.5, 2.0, ((1, 4),), jnp.float32)
    long_taps = normal_values(key_of[5], (KM, CHANNELS), KM ** -0.5, 0.5, ((1, 4),))
    return {"gate_query": gate_query, "gate_key": gate_key, "input_value": input_value, "out_grad": out_grad, "short_taps": short_taps, "long_taps": long_taps}


def window_grads(gate_query, gate_key, input_value, out_grad, short_taps, long_taps):
    tok_len = gate_query.shape[0]
    chan_width = gate_query.shape[1]
    short_len = short_taps.shape[0]
    long_len = long_taps.shape[0]
    padded = jnp.concatenate([jnp.zeros((short_len - 1, chan_width), jnp.float32), input_value.astype(jnp.float32)], axis=0)
    mixed_value = jnp.zeros((tok_len, chan_width), jnp.float32)
    for lag in range(short_len):
        mixed_value = mixed_value + short_taps[lag] * padded[short_len - 1 - lag:short_len - 1 - lag + tok_len]
    mixed_value = mixed_value.astype(jnp.bfloat16)
    gated = (gate_key.astype(jnp.float32) * mixed_value.astype(jnp.float32)).astype(jnp.bfloat16)
    period = tok_len + long_len
    gated_spec = jnp.fft.rfft(gated.astype(jnp.float32), n=period, axis=0)
    taps_spec = jnp.fft.rfft(long_taps.astype(jnp.float32), n=period, axis=0)
    long_out = jnp.fft.irfft(gated_spec * taps_spec, n=period, axis=0)[:tok_len]
    query_grad = (out_grad.astype(jnp.float32) * long_out).astype(jnp.bfloat16)
    mid_grad = (out_grad.astype(jnp.float32) * gate_query.astype(jnp.float32)).astype(jnp.bfloat16)
    mid_spec = jnp.fft.rfft(mid_grad.astype(jnp.float32), n=period, axis=0)
    gated_grad = jnp.fft.irfft(mid_spec * jnp.conj(taps_spec), n=period, axis=0)[:tok_len]
    long_sum = jnp.fft.irfft(mid_spec * jnp.conj(gated_spec), n=period, axis=0)[:long_len]
    key_grad = (gated_grad * mixed_value.astype(jnp.float32)).astype(jnp.bfloat16)
    mixed_grad = (gated_grad * gate_key.astype(jnp.float32)).astype(jnp.bfloat16)
    trailing = jnp.concatenate([mixed_grad.astype(jnp.float32), jnp.zeros((short_len - 1, chan_width), jnp.float32)], axis=0)
    value_grad = jnp.zeros((tok_len, chan_width), jnp.float32)
    for lag in range(short_len):
        value_grad = value_grad + short_taps[lag] * trailing[lag:lag + tok_len]
    value_grad = value_grad.astype(jnp.bfloat16)
    short_sum = jnp.stack([lax.optimization_barrier(jnp.sum(mixed_grad.astype(jnp.float32) * padded[short_len - 1 - lag:short_len - 1 - lag + tok_len], axis=0)) for lag in range(short_len)], axis=0)
    return (query_grad, key_grad, value_grad, long_sum.astype(jnp.float32), short_sum)

def reference(gate_query, gate_key, input_value, out_grad, short_taps, long_taps):

    def one_window(items):
        return window_grads(items[0], items[1], items[2], items[3], short_taps, long_taps)
    query_grad, key_grad, value_grad, long_parts, short_parts = lax.map(one_window, (gate_query, gate_key, input_value, out_grad))
    long_sum = lax.optimization_barrier(jnp.sum(long_parts, axis=0))
    short_sum = lax.optimization_barrier(jnp.sum(short_parts, axis=0))
    norm_sq = jnp.sum(long_sum * long_sum) + jnp.sum(short_sum * short_sum)
    limit = jnp.sqrt(jnp.asarray((KM + KS) * CHANNELS, jnp.float32))
    factor = limit / jnp.sqrt(norm_sq + 1e-06)
    long_grad = (factor * long_sum).astype(jnp.bfloat16)
    short_grad = (factor * short_sum).astype(jnp.bfloat16)
    return (query_grad, key_grad, value_grad, long_grad, short_grad)
```

```python
import math

import jax
import jax.numpy as jnp
import numpy as np
from jax import lax
from jax.experimental import pallas as pl
from jax.experimental.pallas import tpu as pltpu
from jax.sharding import PartitionSpec as P

BF = jnp.bfloat16
F32 = jnp.float32
ROWS = 128
PIECES = 64
WIDTH = 512
VMEM = 48 * 1024 * 1024


def split_table(table):
    high = table.astype(np.float32).astype(jnp.bfloat16)
    low = (table - high.astype(np.float64)).astype(np.float32).astype(jnp.bfloat16)
    return high, low


def tables():
    freq = np.arange(128)[:, None]
    place = np.arange(256)[None, :]
    angle = (freq * place % 256) * (2.0 * np.pi / 256)
    fwd = np.concatenate([np.cos(angle), -np.sin(angle)], axis=0)
    fwd[128] = 1.0 - 2.0 * (np.arange(256) % 2)
    weight = np.full((256,), 2.0 / 256)
    weight[0] = weight[128] = 1.0 / 256
    inv = (fwd * weight[:, None]).T[:ROWS]
    fwd_hi, fwd_lo = split_table(fwd)
    inv_hi, inv_lo = split_table(inv)
    near = np.concatenate([fwd_hi[:, :128], fwd_lo[:, :128]], axis=1)
    far = np.concatenate([fwd_hi[:, 128:], fwd_lo[:, 128:]], axis=1)
    inv_both = np.concatenate([inv_hi, inv_lo], axis=0)
    return fwd_hi, fwd_lo, near, far, inv_both


def half_of(slot, core):
    return jnp.where(core == 0, 1 - slot, slot)


def gate_kernel(core_ref, query_ref, key_ref, value_ref, grad_ref, taps_ref, mid_ref, gated_ref, mixed_ref, wide_ref):
    short_len = taps_ref.shape[0]
    mid_ref[0] = (grad_ref[...].astype(F32) * query_ref[...].astype(F32)).astype(BF)
    wide_ref[0:8, :] = jnp.zeros((8, wide_ref.shape[1]), F32)
    wide_ref[8:, :] = value_ref[...].astype(F32)
    total = taps_ref[0:1, :] * wide_ref[8 : 8 + ROWS, :]
    for lag in range(1, short_len):
        total = total + taps_ref[lag : lag + 1, :] * wide_ref[8 - lag : 8 - lag + ROWS, :]
    mixed = total.astype(BF)
    mixed_ref[0] = mixed
    gated_ref[0] = (key_ref[...].astype(F32) * mixed.astype(F32)).astype(BF)


def head_kernel(core_ref, rim_ref, value_ref, key_ref, taps_ref, mixed_ref, gated_ref, wide_ref):
    short_len = taps_ref.shape[0]
    wide_ref[0:8, :] = rim_ref[...].astype(F32)
    wide_ref[8:, :] = value_ref[...].astype(F32)
    total = taps_ref[0:1, :] * wide_ref[8:24, :]
    for lag in range(1, short_len):
        total = total + taps_ref[lag : lag + 1, :] * wide_ref[8 - lag : 24 - lag, :]
    mixed = total.astype(BF)
    mixed_ref[0] = mixed
    gated_ref[0] = (key_ref[...].astype(F32) * mixed.astype(F32)).astype(BF)


def dot(left, right):
    return jnp.dot(left, right, preferred_element_type=F32)


def product(first, second, conjugate):
    first_re, first_im = first[:128], first[128:]
    second_re, second_im = second[:128], second[128:]
    edge = lax.broadcasted_iota(jnp.int32, first_re.shape, 0) == 0
    cross = first_im * second_im
    inner = jnp.where(edge, 0.0, cross)
    if conjugate:
        real = first_re * second_re + inner
        imag = first_im * second_re - first_re * second_im
    else:
        real = first_re * second_re - inner
        imag = first_re * second_im + first_im * second_re
    return jnp.concatenate([real, jnp.where(edge, cross, imag)], axis=0)


def inverse(inv_ref, spec):
    high = spec.astype(BF)
    low = (spec - high.astype(F32)).astype(BF)
    both = dot(inv_ref[...], high)
    return both[:ROWS] + both[ROWS:] + dot(inv_ref[0:ROWS, :], low)


def filter_kernel(
    core_ref, gated_ref, gated_head_ref, prev_ref, prev_head_ref, mid_ref, next_ref, mixed_ref, mixed_head_ref,
    key_ref, value_ref, rim_ref, grad_ref, short_ref, long_ref, hi_ref, lo_ref, near_ref, far_ref, inv_ref, *rest,
):
    query_out, key_out, value_out, top_out, end_out, part_ref, wide_ref, mixed_grad_ref = rest[-8:]
    short_len = short_ref.shape[0]
    width = wide_ref.shape[1]
    gated = jnp.concatenate([gated_head_ref[0], gated_ref[0, 16:], prev_head_ref[0], prev_ref[0, 16:]], axis=0)
    mid = mid_ref[0]
    ahead = next_ref[0]
    taps = long_ref[...]
    gated_spec = dot(hi_ref[...], gated) + dot(lo_ref[...], gated)
    mid_spec = dot(near_ref[...], jnp.concatenate([mid, mid], axis=0))
    both_spec = mid_spec + dot(far_ref[...], jnp.concatenate([ahead, ahead], axis=0))
    taps_spec = dot(near_ref[...], jnp.concatenate([taps, taps], axis=0))
    long_sum = inverse(inv_ref, product(mid_spec, gated_spec, True))
    gated_grad = inverse(inv_ref, product(both_spec, taps_spec, True))
    long_out = inverse(inv_ref, product(gated_spec, taps_spec, False))
    query_out[...] = (grad_ref[...].astype(F32) * long_out).astype(BF)
    mixed = jnp.concatenate([mixed_head_ref[0], mixed_ref[0, 16:]], axis=0)
    key_out[...] = (gated_grad * mixed.astype(F32)).astype(BF)
    mixed_grad = (gated_grad * key_ref[...].astype(F32)).astype(BF)
    top_out[...] = mixed_grad[0:16]
    end_out[...] = mixed_grad[ROWS - 16 :]
    mixed_grad = mixed_grad.astype(F32)
    mixed_grad_ref[0:ROWS, :] = mixed_grad
    mixed_grad_ref[ROWS:, :] = jnp.zeros((8, width), F32)
    wide_ref[0:8, :] = rim_ref[...].astype(F32)
    wide_ref[8:, :] = value_ref[...].astype(F32)
    total = short_ref[0:1, :] * mixed_grad
    sums = [jnp.sum(mixed_grad * wide_ref[8 : 8 + ROWS, :], axis=0, keepdims=True)]
    for lag in range(1, short_len):
        total = total + short_ref[lag : lag + 1, :] * mixed_grad_ref[lag : lag + ROWS, :]
        sums.append(jnp.sum(mixed_grad * wide_ref[8 - lag : 8 - lag + ROWS, :], axis=0, keepdims=True))
    value_out[...] = total.astype(BF)
    short_sum = jnp.concatenate(sums + [jnp.zeros((16 - short_len, width), F32)], axis=0)
    for block in range(width // 128):
        lanes = slice(block * 128, block * 128 + 128)
        part_ref[block, 0:ROWS, :] = long_sum[:, lanes].astype(part_ref.dtype)
        part_ref[block, ROWS : ROWS + 16, :] = short_sum[:, lanes].astype(part_ref.dtype)


def tail_kernel(end_ref, rim_ref, taps_ref, old_ref, out_ref, wide_ref):
    short_len = taps_ref.shape[0]
    wide_ref[0:16, :] = end_ref[...].astype(F32)
    wide_ref[16:, :] = rim_ref[...].astype(F32)
    total = taps_ref[0:1, :] * wide_ref[0:16, :]
    for lag in range(1, short_len):
        total = total + taps_ref[lag : lag + 1, :] * wide_ref[lag : lag + 16, :]
    out_ref[...] = total.astype(BF)


def params():
    return pltpu.CompilerParams(vmem_limit_bytes=VMEM)


def shifted(value, by):
    devices = lax.axis_size("ctx")
    return lax.ppermute(value, "ctx", [(i, i + by) for i in range(devices) if 0 <= i + by < devices])


def on_device(gate_query, gate_key, input_value, out_grad, short_taps, long_taps):
    query_rows, key_rows, value_rows, grad_rows = gate_query[0], gate_key[0], input_value[0], out_grad[0]
    chan_width = query_rows.shape[1]
    half_width = chan_width // 2
    short_len, long_len = short_taps.shape[0], long_taps.shape[0]
    core = lax.axis_index("dp").astype(jnp.int32).reshape(1)
    devices = lax.axis_size("ctx")
    per_half = half_width // WIDTH
    struct = jax.ShapeDtypeStruct

    value_rim = shifted(value_rows[ROWS - 8 :], 1)

    def slot_map(i, core):
        return (half_of(i // per_half, core[0]), 0, i % per_half)

    whole = pl.BlockSpec((ROWS, WIDTH), lambda i, core: (0, i))
    by_slot = pl.BlockSpec((1, ROWS, WIDTH), slot_map)
    halves = struct((2, ROWS, half_width), BF)
    mid, gated, mixed = pl.pallas_call(
        gate_kernel,
        out_shape=(halves, halves, halves),
        grid_spec=pltpu.PrefetchScalarGridSpec(
            num_scalar_prefetch=1,
            grid=(chan_width // WIDTH,),
            in_specs=[whole, whole, whole, whole, pl.BlockSpec((short_len, WIDTH), lambda i, core: (0, i))],
            out_specs=[by_slot, by_slot, by_slot],
            scratch_shapes=[pltpu.VMEM((ROWS + 8, WIDTH), F32)],
        ),
        compiler_params=params(),
        name="gates",
    )(core, query_rows, key_rows, value_rows, grad_rows, short_taps)

    prev_parts = [shifted(gated[slot], 1) for slot in range(2)]
    next_parts = [shifted(mid[slot], -1) for slot in range(2)]

    head_in = pl.BlockSpec((16, WIDTH), lambda i, core: (0, i))
    head_out = pl.BlockSpec((1, 16, WIDTH), slot_map)
    heads = struct((2, 16, half_width), BF)
    mixed_head, gated_head = pl.pallas_call(
        head_kernel,
        out_shape=(heads, heads),
        grid_spec=pltpu.PrefetchScalarGridSpec(
            num_scalar_prefetch=1,
            grid=(chan_width // WIDTH,),
            in_specs=[
                pl.BlockSpec((8, WIDTH), lambda i, core: (0, i)),
                head_in,
                head_in,
                pl.BlockSpec((short_len, WIDTH), lambda i, core: (0, i)),
            ],
            out_specs=[head_out, head_out],
            scratch_shapes=[pltpu.VMEM((24, WIDTH), F32)],
        ),
        compiler_params=params(),
        name="head",
    )(core, value_rim, value_rows, key_rows, short_taps)
    prev_head = shifted(gated_head, 1)

    fwd_hi, fwd_lo, near, far, inv_both = (jnp.asarray(t) for t in tables())

    def run_filter(slot, kept):
        def chan(rows):
            return pl.BlockSpec((rows, WIDTH), lambda i, core: (0, half_of(slot, core[0]) * per_half + i))

        def held(rows):
            return pl.BlockSpec((1, rows, WIDTH), lambda i, core: (slot, 0, i))

        sent = pl.BlockSpec((1, ROWS, WIDTH), lambda i, core: (0, 0, i))
        table = pl.BlockSpec((256, 256), lambda i, core: (0, 0))
        wide = struct((ROWS, chan_width), BF)
        rim = struct((16, chan_width), BF)
        part = struct((half_width // 128, ROWS + 16, 128), BF if slot == 0 else F32)
        in_specs = [
            held(ROWS), held(16), sent, held(16), held(ROWS), sent, held(ROWS), held(16),
            chan(ROWS), chan(ROWS), chan(8), chan(ROWS), chan(short_len), chan(long_len),
            table, table, table, table, table,
        ]
        first = 1 + len(in_specs)
        return pl.pallas_call(
            filter_kernel,
            out_shape=(wide, wide, wide, rim, rim, part),
            grid_spec=pltpu.PrefetchScalarGridSpec(
                num_scalar_prefetch=1,
                grid=(per_half,),
                in_specs=in_specs + [pl.BlockSpec(memory_space=pl.ANY)] * len(kept),
                out_specs=[
                    chan(ROWS), chan(ROWS), chan(ROWS), chan(16), chan(16),
                    pl.BlockSpec((WIDTH // 128, ROWS + 16, 128), lambda i, core: (i, 0, 0)),
                ],
                scratch_shapes=[pltpu.VMEM((ROWS + 8, WIDTH), F32), pltpu.VMEM((ROWS + 8, WIDTH), F32)],
            ),
            input_output_aliases={first + k: k for k in range(len(kept))},
            compiler_params=params(),
            name=f"filters_{slot}",
        )(
            core, gated, gated_head, prev_parts[slot][None], prev_head, mid, next_parts[slot][None], mixed, mixed_head,
            key_rows, value_rows, value_rim, grad_rows, short_taps, long_taps, fwd_hi, fwd_lo, near, far, inv_both, *kept,
        )

    *kept, part_sent = run_filter(0, ())
    part_got = lax.ppermute(part_sent, "dp", [(0, 1), (1, 0)])
    query_grad, key_grad, value_grad, mixed_top, mixed_end, part_own = run_filter(1, tuple(kept))

    blocks = half_width // 128
    groups = PIECES // blocks
    total = part_own + part_got.astype(F32)
    long_part = total[:, :ROWS].reshape(blocks, groups, ROWS // groups, 128)
    short_part = total[:, ROWS : ROWS + groups].reshape(blocks, groups, 1, 128)
    pieces = jnp.concatenate([long_part, short_part], axis=2).astype(BF)
    depth = pieces.shape[2]
    owned = PIECES // devices
    arrived = lax.all_to_all(pieces.reshape(PIECES, depth, 128), "ctx", 0, 0, tiled=True)
    summed = jnp.sum(arrived.reshape(devices, owned, depth, 128).astype(F32), axis=0)
    square = jnp.sum(summed * summed, axis=(1, 2), keepdims=True)
    high = square.astype(BF)
    low = (square - high.astype(F32)).astype(BF)
    line = (owned, 1, 128)
    message = jnp.concatenate([summed.astype(BF), jnp.broadcast_to(high, line), jnp.broadcast_to(low, line)], axis=1)
    spread = jnp.broadcast_to(message[None], (devices,) + message.shape).reshape(PIECES, depth + 2, 128)
    gathered = lax.all_to_all(spread, "ctx", 0, 0, tiled=True)
    gathered = lax.all_gather(gathered, "dp")
    gathered = gathered.reshape(2, blocks, groups, depth + 2, 128)
    local_sq = jnp.sum(gathered[:, :, :, depth:, 0].astype(F32))
    ways = lax.axis_size("tp")
    norms = lax.all_to_all(jnp.full((ways, 8, 128), local_sq, F32), "tp", 0, 0, tiled=True)
    norm_sq = jnp.sum(norms[:, 0, 0])
    limit = math.sqrt((long_len + short_len) * chan_width * ways)
    factor = limit / jnp.sqrt(norm_sq + 1e-06)
    long_total = gathered[:, :, :, : depth - 1].transpose(2, 3, 0, 1, 4).reshape(long_len, chan_width)
    short_total = gathered[:, :, :, depth - 1].transpose(2, 0, 1, 3).reshape(groups, chan_width)[:short_len]
    long_grad = (factor * long_total.astype(F32)).astype(BF)
    short_grad = (factor * short_total.astype(F32)).astype(BF)

    mixed_rim = shifted(mixed_top, -1)
    value_grad = pl.pallas_call(
        tail_kernel,
        out_shape=struct((ROWS, chan_width), BF),
        grid=(1,),
        in_specs=[
            pl.BlockSpec((16, chan_width), lambda i: (0, 0)),
            pl.BlockSpec((16, chan_width), lambda i: (0, 0)),
            pl.BlockSpec((short_len, chan_width), lambda i: (0, 0)),
            pl.BlockSpec(memory_space=pl.ANY),
        ],
        out_specs=pl.BlockSpec((16, chan_width), lambda i: (ROWS // 16 - 1, 0)),
        scratch_shapes=[pltpu.VMEM((32, chan_width), F32)],
        input_output_aliases={3: 0},
        compiler_params=params(),
        name="tail",
    )(mixed_end, mixed_rim, short_taps, value_grad)
    return (query_grad[None], key_grad[None], value_grad[None], long_grad, short_grad)


def solution(mesh):
    split = P("dp", "ctx", "tp")
    taps = P(None, "tp")
    return jax.shard_map(
        on_device,
        mesh=mesh,
        in_specs=(split, split, split, split, taps, taps),
        out_specs=(split, split, split, taps, taps),
        check_vma=False,
    )
```

```python
import functools
import math

import jax
import jax.numpy as jnp
import numpy as np
from jax import lax
from jax.experimental import pallas as pl
from jax.experimental.pallas import tpu as pltpu
from jax.sharding import PartitionSpec as P

BF = jnp.bfloat16
F32 = jnp.float32
ROWS = 128
PIECES = 64
WIDTH = 512
VMEM = 60 * 1024 * 1024


def split_table(table):
    high = table.astype(np.float32).astype(jnp.bfloat16)
    low = (table - high.astype(np.float64)).astype(np.float32).astype(jnp.bfloat16)
    return high, low


def tables():
    freq = np.arange(128)[:, None]
    place = np.arange(256)[None, :]
    angle = (freq * place % 256) * (2.0 * np.pi / 256)
    fwd = np.concatenate([np.cos(angle), -np.sin(angle)], axis=0)
    fwd[128] = 1.0 - 2.0 * (np.arange(256) % 2)
    weight = np.full((256,), 2.0 / 256)
    weight[0] = weight[128] = 1.0 / 256
    inv = (fwd * weight[:, None]).T
    fwd_hi, fwd_lo = split_table(fwd)
    inv_hi, inv_lo = split_table(inv)
    near = np.concatenate([fwd_hi[:, :128], fwd_lo[:, :128]], axis=1)
    away = np.concatenate([fwd_hi[:, 128:], fwd_lo[:, 128:]], axis=1)
    inv_both = np.concatenate([inv_hi[:ROWS], inv_lo[:ROWS]], axis=0)
    return fwd_hi, fwd_lo, near, away, inv_both


def half_of(slot, core):
    return jnp.where(core == 0, 1 - slot, slot)


def gate_kernel(query_ref, key_ref, value_ref, grad_ref, taps_ref, up_ref, down_ref, mixed_ref, wide_ref):
    short_len = taps_ref.shape[0]
    width = wide_ref.shape[1]
    down_ref[...] = (grad_ref[...].astype(F32) * query_ref[...].astype(F32)).astype(BF)
    wide_ref[0:8, :] = jnp.zeros((8, width), F32)
    wide_ref[8:, :] = value_ref[...].astype(F32)
    total = taps_ref[0:1, :] * wide_ref[8 : 8 + ROWS, :]
    for lag in range(1, short_len):
        total = total + taps_ref[lag : lag + 1, :] * wide_ref[8 - lag : 8 - lag + ROWS, :]
    mixed = total.astype(BF)
    mixed_ref[...] = mixed
    gated = key_ref[...].astype(F32) * mixed.astype(F32)
    row = lax.broadcasted_iota(jnp.int32, (8, width), 0)
    wide_ref[0:16, :] = gated[0:16]
    top = jnp.where(row < 2, wide_ref[6:14, :], wide_ref[ROWS : ROWS + 8, :])
    up_ref[0:16, :] = jnp.concatenate([top, gated[8:16]], axis=0).astype(BF)
    up_ref[16:ROWS, :] = gated[16:].astype(BF)


def own_head(wide_ref, tail, key_ref, value_ref, taps_ref):
    value = value_ref[0:16, :].astype(F32)[0:8]
    key = key_ref[0:16, :].astype(F32)[0:8]
    wide_ref[0:8, :] = tail
    wide_ref[8:16, :] = value
    total = taps_ref[0:1, :] * value
    for lag in range(1, taps_ref.shape[0]):
        total = total + taps_ref[lag : lag + 1, :] * wide_ref[8 - lag : 16 - lag, :]
    mixed = total.astype(BF).astype(F32)
    return mixed, (key * mixed).astype(BF).astype(F32)


def with_heads(own_head_rows, up_ref, got_head_rows, got_ref):
    parts = []
    for head, ref in ((own_head_rows, up_ref), (got_head_rows, got_ref)):
        parts.append(jnp.concatenate([head, ref[0:16, :].astype(F32)[8:16]], axis=0).astype(BF))
        parts.append(ref[16:ROWS, :])
    return jnp.concatenate(parts, axis=0)


def dot(left, right):
    return jnp.dot(left, right, preferred_element_type=F32)


def product(first, second, conjugate):
    first_re, first_im = first[:128], first[128:]
    second_re, second_im = second[:128], second[128:]
    edge = lax.broadcasted_iota(jnp.int32, first_re.shape, 0) == 0
    cross = first_im * second_im
    inner = jnp.where(edge, 0.0, cross)
    if conjugate:
        real = first_re * second_re + inner
        imag = first_im * second_re - first_re * second_im
    else:
        real = first_re * second_re - inner
        imag = first_re * second_im + first_im * second_re
    return jnp.concatenate([real, jnp.where(edge, cross, imag)], axis=0)


def inverse(inv_ref, spec):
    high = spec.astype(BF)
    low = (spec - high.astype(F32)).astype(BF)
    both = dot(inv_ref[...], high)
    return both[:ROWS] + both[ROWS:] + dot(inv_ref[0:ROWS, :], low)


def twice(rows):
    return jnp.concatenate([rows, rows], axis=0)


def sums_kernel(
    core_ref, up_ref, got_ref, down_ref, back_ref, mixed_ref, key_ref, value_ref, short_ref, long_ref,
    hi_ref, lo_ref, near_ref, away_ref, inv_ref, *rest,
):
    key_out, mixed_out, gated_top_out, mixed_top_out, part_ref, wide_ref = rest[-6:]
    short_len = short_ref.shape[0]
    width = wide_ref.shape[1]
    row = lax.broadcasted_iota(jnp.int32, (8, width), 0)
    got_top = got_ref[0:16, :].astype(F32)[0:8]
    mixed_top, gated_top = own_head(wide_ref, got_top, key_ref, value_ref, short_ref)
    gated_top_out[...] = gated_top.astype(BF)
    wide_ref[8:16, :] = got_top
    before = jnp.where(row < 6, 0.0, wide_ref[2:10, :])
    gated = with_heads(gated_top, up_ref, before, got_ref)
    mid = down_ref[...]
    ahead = back_ref[...]
    gated_spec = dot(hi_ref[...], gated) + dot(lo_ref[...], gated)
    mid_spec = dot(near_ref[...], twice(mid))
    both_spec = mid_spec + dot(away_ref[...], twice(ahead))
    taps_spec = dot(near_ref[...], twice(long_ref[...]))
    long_sum = inverse(inv_ref, product(mid_spec, gated_spec, True))
    gated_grad = inverse(inv_ref, product(both_spec, taps_spec, True))
    next_top = back_ref[0:16, :].astype(F32)[0:8]
    lines = [jnp.zeros((3, width), F32)]
    for gap in range(5, 0, -1):
        line = gated_top[gap : gap + 1] * next_top[0:1]
        for r in range(gap + 1, 6):
            line = line + gated_top[r : r + 1] * next_top[r - gap : r - gap + 1]
        lines.append(line)
    long_end = long_sum[ROWS - 8 :] + jnp.concatenate(lines, axis=0)
    long_sum = jnp.concatenate([long_sum[: ROWS - 8], long_end], axis=0)
    mixed = jnp.concatenate([mixed_top, mixed_ref[0:16, :].astype(F32)[8:16], mixed_ref[16:, :].astype(F32)], axis=0)
    key_out[...] = (gated_grad * mixed).astype(BF)
    mixed_grad = (gated_grad * key_ref[...].astype(F32)).astype(BF)
    mixed_out[...] = mixed_grad
    mixed_grad = mixed_grad.astype(F32)
    mixed_top_out[...] = mixed_grad[0:8].astype(BF)
    wide_ref[0:8, :] = got_top
    wide_ref[8:, :] = value_ref[...].astype(F32)
    sums = []
    for lag in range(short_len):
        sums.append(jnp.sum(mixed_grad * wide_ref[8 - lag : 8 - lag + ROWS, :], axis=0, keepdims=True))
    short_sum = jnp.concatenate(sums + [jnp.zeros((16 - short_len, width), F32)], axis=0)
    for block in range(width // 128):
        lanes = slice(block * 128, block * 128 + 128)
        part_ref[block, 0:ROWS, :] = long_sum[:, lanes].astype(part_ref.dtype)
        part_ref[block, ROWS : ROWS + 16, :] = short_sum[:, lanes].astype(part_ref.dtype)


def rest_kernel(
    up_ref, got_ref, gated_top_ref, before_ref, grad_ref, mixed_ref, rim_ref, short_ref, long_ref,
    hi_ref, lo_ref, near_ref, inv_ref, query_out, value_out, wide_ref,
):
    gated = with_heads(gated_top_ref[...].astype(F32), up_ref, before_ref[...].astype(F32), got_ref)
    gated_spec = dot(hi_ref[...], gated) + dot(lo_ref[...], gated)
    taps_spec = dot(near_ref[...], twice(long_ref[...]))
    long_out = inverse(inv_ref, product(gated_spec, taps_spec, False))
    query_out[...] = (grad_ref[...].astype(F32) * long_out).astype(BF)
    wide_ref[0:ROWS, :] = mixed_ref[...].astype(F32)
    wide_ref[ROWS:, :] = rim_ref[...].astype(F32)
    total = short_ref[0:1, :] * wide_ref[0:ROWS, :]
    for lag in range(1, short_ref.shape[0]):
        total = total + short_ref[lag : lag + 1, :] * wide_ref[lag : lag + ROWS, :]
    value_out[...] = total.astype(BF)


def piece_kernel(arrived_ref, spread_ref):
    total = arrived_ref[0].astype(F32)
    for device in range(1, arrived_ref.shape[0]):
        total = total + arrived_ref[device].astype(F32)
    square = jnp.sum(jnp.sum(total * total, axis=2, keepdims=True), axis=1, keepdims=True)
    square = jnp.broadcast_to(square, (total.shape[0], 1, total.shape[2]))
    high = square.astype(BF).astype(F32)
    message = jnp.concatenate([total, high, square - high], axis=1).astype(BF)
    for device in range(spread_ref.shape[0]):
        spread_ref[device] = message


def norm_kernel(pieces_ref, norm_ref):
    depth = pieces_ref.shape[1]
    total = pieces_ref[0].astype(F32)
    for piece in range(1, pieces_ref.shape[0]):
        total = total + pieces_ref[piece].astype(F32)
    square = total[depth - 2 : depth - 1] + total[depth - 1 : depth]
    norm_ref[...] = jnp.broadcast_to(square[None], norm_ref.shape)


def scale_kernel(limit, core_ref, mine_ref, other_ref, norms_ref, long_ref, short_ref):
    norm_sq = norms_ref[0]
    for device in range(1, norms_ref.shape[0]):
        norm_sq = norm_sq + norms_ref[device]
    factor = (limit / jnp.sqrt(norm_sq + 1e-06))[0:1]
    short_len = short_ref.shape[0]
    blocks = long_ref.shape[1] // 128
    groups = mine_ref.shape[0] // blocks
    rows = ROWS // groups

    def write(pieces_ref):
        for block in range(blocks):
            lanes = slice(block * 128, block * 128 + 128)
            lines = []
            for group in range(groups):
                piece = pieces_ref[block * groups + group].astype(F32) * factor
                long_ref[group * rows : group * rows + rows, lanes] = piece[:rows].astype(BF)
                lines.append(piece[rows : rows + 1])
            short_ref[:, lanes] = jnp.concatenate(lines, axis=0)[:short_len].astype(BF)

    @pl.when(pl.program_id(0) == 0)
    def _():
        write(mine_ref)

    @pl.when(pl.program_id(0) == 1)
    def _():
        write(other_ref)


def params():
    return pltpu.CompilerParams(vmem_limit_bytes=VMEM)


def shifted(value, by):
    devices = lax.axis_size("ctx")
    return lax.ppermute(value, "ctx", [(i, i + by) for i in range(devices) if 0 <= i + by < devices])


def on_device(gate_query, gate_key, input_value, out_grad, short_taps, long_taps):
    query_rows, key_rows, value_rows, grad_rows = gate_query[0], gate_key[0], input_value[0], out_grad[0]
    chan_width = query_rows.shape[1]
    half_width = chan_width // 2
    short_len, long_len = short_taps.shape[0], long_taps.shape[0]
    core = lax.axis_index("dp").astype(jnp.int32).reshape(1)
    devices = lax.axis_size("ctx")
    per_half = half_width // WIDTH
    struct = jax.ShapeDtypeStruct
    count = chan_width // WIDTH

    def chan(rows):
        return pl.BlockSpec((rows, WIDTH), lambda i: (0, i))

    wide = struct((ROWS, chan_width), BF)
    top = struct((8, chan_width), BF)
    up, down, mixed = pl.pallas_call(
        gate_kernel,
        out_shape=(wide, wide, wide),
        grid=(count,),
        in_specs=[chan(ROWS), chan(ROWS), chan(ROWS), chan(ROWS), chan(short_len)],
        out_specs=[chan(ROWS), chan(ROWS), chan(ROWS)],
        scratch_shapes=[pltpu.VMEM((ROWS + 8, WIDTH), F32)],
        compiler_params=params(),
        name="gates",
    )(query_rows, key_rows, value_rows, grad_rows, short_taps)
    got = shifted(up, 1)
    back = shifted(down, -1)

    fwd_hi, fwd_lo, near, away, inv_both = (jnp.asarray(t) for t in tables())

    def run_sums(slot, kept):
        def half(rows):
            return pl.BlockSpec((rows, WIDTH), lambda i, core: (0, half_of(slot, core[0]) * per_half + i))

        table = pl.BlockSpec((256, 256), lambda i, core: (0, 0))
        part = struct((half_width // 128, ROWS + 16, 128), BF if slot == 0 else F32)
        in_specs = [half(ROWS)] * 7 + [half(short_len), half(long_len)] + [table] * 5
        first = 1 + len(in_specs)
        return pl.pallas_call(
            sums_kernel,
            out_shape=(wide, wide, top, top, part),
            grid_spec=pltpu.PrefetchScalarGridSpec(
                num_scalar_prefetch=1,
                grid=(per_half,),
                in_specs=in_specs + [pl.BlockSpec(memory_space=pl.ANY)] * len(kept),
                out_specs=[
                    half(ROWS), half(ROWS), half(8), half(8),
                    pl.BlockSpec((WIDTH // 128, ROWS + 16, 128), lambda i, core: (i, 0, 0)),
                ],
                scratch_shapes=[pltpu.VMEM((ROWS + 8, WIDTH), F32)],
            ),
            input_output_aliases={first + k: k for k in range(len(kept))},
            compiler_params=params(),
            cost_estimate=pl.CostEstimate(flops=2_000_000_000, bytes_accessed=4_000_000, transcendentals=0),
            name=f"sums_{slot}",
        )(
            core, up, got, down, back, mixed, key_rows, value_rows, short_taps, long_taps,
            fwd_hi, fwd_lo, near, away, inv_both, *kept,
        )

    *kept, part_sent = run_sums(0, ())
    part_got = lax.ppermute(part_sent, "dp", [(0, 1), (1, 0)])
    key_grad, mixed_grad, gated_top, mixed_top, part_own = run_sums(1, tuple(kept))

    blocks = half_width // 128
    groups = PIECES // blocks
    total = part_own + part_got.astype(F32)
    long_part = total[:, :ROWS].reshape(blocks, groups, ROWS // groups, 128)
    short_part = total[:, ROWS : ROWS + groups].reshape(blocks, groups, 1, 128)
    pieces = jnp.concatenate([long_part, short_part], axis=2).astype(BF)
    depth = pieces.shape[2]
    owned = PIECES // devices
    arrived = lax.all_to_all(pieces.reshape(PIECES, depth, 128), "ctx", 0, 0, tiled=True)
    spread = pl.pallas_call(
        piece_kernel,
        out_shape=struct((devices, owned, depth + 2, 128), BF),
        compiler_params=params(),
        name="piece",
    )(arrived.reshape(devices, owned, depth, 128))
    spread, gated_top, mixed_top = lax.optimization_barrier((spread, gated_top, mixed_top))
    gathered = lax.all_to_all(spread.reshape(PIECES, depth + 2, 128), "ctx", 0, 0, tiled=True)
    before = shifted(gated_top, 1)
    rim = shifted(mixed_top, -1)
    table = pl.BlockSpec((256, 256), lambda i: (0, 0))
    query_grad, value_grad = pl.pallas_call(
        rest_kernel,
        out_shape=(wide, wide),
        grid=(count,),
        in_specs=[
            chan(ROWS), chan(ROWS), chan(8), chan(8), chan(ROWS), chan(ROWS), chan(8),
            chan(short_len), chan(long_len), table, table, table, table,
        ],
        out_specs=[chan(ROWS), chan(ROWS)],
        scratch_shapes=[pltpu.VMEM((ROWS + 8, WIDTH), F32)],
        compiler_params=params(),
        cost_estimate=pl.CostEstimate(flops=4_000_000_000, bytes_accessed=5_000_000, transcendentals=0),
        name="rest",
    )(
        up, got, gated_top, before, grad_rows, mixed_grad, rim, short_taps, long_taps,
        fwd_hi, fwd_lo, near, inv_both,
    )

    ways = lax.axis_size("tp")
    norms = pl.pallas_call(
        norm_kernel,
        out_shape=struct((2 * ways, 1, 128), F32),
        compiler_params=params(),
        name="norm",
    )(gathered)
    norms = lax.all_to_all(norms, ("tp", "dp"), 0, 0, tiled=True)
    other = lax.ppermute(gathered, "dp", [(0, 1), (1, 0)])
    limit = math.sqrt((long_len + short_len) * chan_width * ways)
    whole = pl.BlockSpec((PIECES, depth + 2, 128), lambda i, core: (0, 0, 0))

    def result(rows):
        return pl.BlockSpec((rows, half_width), lambda i, core: (0, jnp.where(i == 0, core[0], 1 - core[0])))

    long_grad, short_grad = pl.pallas_call(
        functools.partial(scale_kernel, limit),
        out_shape=(struct((long_len, chan_width), BF), struct((short_len, chan_width), BF)),
        grid_spec=pltpu.PrefetchScalarGridSpec(
            num_scalar_prefetch=1,
            grid=(2,),
            in_specs=[whole, whole, pl.BlockSpec((2 * ways, 1, 128), lambda i, core: (0, 0, 0))],
            out_specs=[result(long_len), result(short_len)],
        ),
        compiler_params=params(),
        name="scale",
    )(core, gathered, other, norms)
    return (query_grad[None], key_grad[None], value_grad[None], long_grad, short_grad)


def solution(mesh):
    split = P("dp", "ctx", "tp")
    taps = P(None, "tp")
    return jax.shard_map(
        on_device,
        mesh=mesh,
        in_specs=(split, split, split, split, taps, taps),
        out_specs=(split, split, split, taps, taps),
        check_vma=False,
    )
```

```python
import functools
import math

import jax
import jax.numpy as jnp
import numpy as np
from jax import lax
from jax.experimental import pallas as pl
from jax.experimental.pallas import tpu as pltpu
from jax.sharding import PartitionSpec as P

BF = jnp.bfloat16
F32 = jnp.float32
ROWS = 128
WIDTH = 512
VMEM = 60 * 1024 * 1024
SMALL = 16 * 1024 * 1024


def split_table(table):
    high = table.astype(np.float32).astype(jnp.bfloat16)
    low = (table - high.astype(np.float64)).astype(np.float32).astype(jnp.bfloat16)
    return high, low


def tables():
    freq = np.arange(128)[:, None]
    place = np.arange(256)[None, :]
    angle = (freq * place % 256) * (2.0 * np.pi / 256)
    fwd = np.concatenate([np.cos(angle), -np.sin(angle)], axis=0)
    fwd[128] = 1.0 - 2.0 * (np.arange(256) % 2)
    weight = np.full((256,), 2.0 / 256)
    weight[0] = weight[128] = 1.0 / 256
    inv = (fwd * weight[:, None]).T
    fwd_hi, fwd_lo = split_table(fwd)
    inv_hi, inv_lo = split_table(inv)
    near = np.concatenate([fwd_hi[:, :128], fwd_lo[:, :128]], axis=1)
    away = np.concatenate([fwd_hi[:, 128:], fwd_lo[:, 128:]], axis=1)
    inv_both = np.concatenate([inv_hi[:ROWS], inv_lo[:ROWS]], axis=0)
    return fwd_hi, fwd_lo, near, away, inv_both


def half_of(slot, core):
    return jnp.where(core == 0, 1 - slot, slot)


def gate_kernel(query_ref, key_ref, value_ref, grad_ref, taps_ref, up_ref, down_ref, mixed_ref, wide_ref):
    short_len = taps_ref.shape[0]
    width = wide_ref.shape[1]
    down_ref[...] = (grad_ref[...].astype(F32) * query_ref[...].astype(F32)).astype(BF)
    wide_ref[0:8, :] = jnp.zeros((8, width), F32)
    wide_ref[8:, :] = value_ref[...].astype(F32)
    total = taps_ref[0:1, :] * wide_ref[8 : 8 + ROWS, :]
    for lag in range(1, short_len):
        total = total + taps_ref[lag : lag + 1, :] * wide_ref[8 - lag : 8 - lag + ROWS, :]
    mixed = total.astype(BF)
    mixed_ref[...] = mixed
    gated = key_ref[...].astype(F32) * mixed.astype(F32)
    row = lax.broadcasted_iota(jnp.int32, (8, width), 0)
    wide_ref[0:16, :] = gated[0:16]
    top = jnp.where(row < 2, wide_ref[6:14, :], wide_ref[ROWS : ROWS + 8, :])
    up_ref[0:16, :] = jnp.concatenate([top, gated[8:16]], axis=0).astype(BF)
    up_ref[16:ROWS, :] = gated[16:].astype(BF)


def own_head(wide_ref, tail, key_ref, value_ref, taps_ref):
    value = value_ref[0:16, :].astype(F32)[0:8]
    key = key_ref[0:16, :].astype(F32)[0:8]
    wide_ref[0:8, :] = tail
    wide_ref[8:16, :] = value
    total = taps_ref[0:1, :] * value
    for lag in range(1, taps_ref.shape[0]):
        total = total + taps_ref[lag : lag + 1, :] * wide_ref[8 - lag : 16 - lag, :]
    mixed = total.astype(BF).astype(F32)
    return mixed, (key * mixed).astype(BF).astype(F32)


def with_heads(own_head_rows, up_ref, got_head_rows, got_ref):
    parts = []
    for head, ref in ((own_head_rows, up_ref), (got_head_rows, got_ref)):
        parts.append(jnp.concatenate([head, ref[0:16, :].astype(F32)[8:16]], axis=0).astype(BF))
        parts.append(ref[16:ROWS, :])
    return jnp.concatenate(parts, axis=0)


def dot(left, right):
    return jnp.dot(left, right, preferred_element_type=F32)


def product(first, second, conjugate):
    first_re, first_im = first[:128], first[128:]
    second_re, second_im = second[:128], second[128:]
    edge = lax.broadcasted_iota(jnp.int32, first_re.shape, 0) == 0
    cross = first_im * second_im
    inner = jnp.where(edge, 0.0, cross)
    if conjugate:
        real = first_re * second_re + inner
        imag = first_im * second_re - first_re * second_im
    else:
        real = first_re * second_re - inner
        imag = first_re * second_im + first_im * second_re
    return jnp.concatenate([real, jnp.where(edge, cross, imag)], axis=0)


def inverse(inv_ref, spec):
    high = spec.astype(BF)
    low = (spec - high.astype(F32)).astype(BF)
    both = dot(inv_ref[...], high)
    return both[:ROWS] + both[ROWS:] + dot(inv_ref[0:ROWS, :], low)


def twice(rows):
    return jnp.concatenate([rows, rows], axis=0)


def sums_kernel(
    core_ref, up_ref, got_ref, down_ref, back_ref, mixed_ref, key_ref, value_ref, short_ref, long_ref,
    hi_ref, lo_ref, near_ref, away_ref, inv_ref, *rest,
):
    key_out, mixed_out, gated_top_out, mixed_top_out, part_ref, wide_ref = rest[-6:]
    short_len = short_ref.shape[0]
    width = wide_ref.shape[1]
    row = lax.broadcasted_iota(jnp.int32, (8, width), 0)
    got_top = got_ref[0:16, :].astype(F32)[0:8]
    mixed_top, gated_top = own_head(wide_ref, got_top, key_ref, value_ref, short_ref)
    gated_top_out[...] = gated_top.astype(BF)
    wide_ref[8:16, :] = got_top
    before = jnp.where(row < 6, 0.0, wide_ref[2:10, :])
    gated = with_heads(gated_top, up_ref, before, got_ref)
    mid = down_ref[...]
    ahead = back_ref[...]
    gated_spec = dot(hi_ref[...], gated) + dot(lo_ref[...], gated)
    mid_spec = dot(near_ref[...], twice(mid))
    both_spec = mid_spec + dot(away_ref[...], twice(ahead))
    taps_spec = dot(near_ref[...], twice(long_ref[...]))
    long_sum = inverse(inv_ref, product(mid_spec, gated_spec, True))
    gated_grad = inverse(inv_ref, product(both_spec, taps_spec, True))
    next_top = back_ref[0:16, :].astype(F32)[0:8]
    lines = [jnp.zeros((3, width), F32)]
    for gap in range(5, 0, -1):
        line = gated_top[gap : gap + 1] * next_top[0:1]
        for r in range(gap + 1, 6):
            line = line + gated_top[r : r + 1] * next_top[r - gap : r - gap + 1]
        lines.append(line)
    long_end = long_sum[ROWS - 8 :] + jnp.concatenate(lines, axis=0)
    long_sum = jnp.concatenate([long_sum[: ROWS - 8], long_end], axis=0)
    mixed = jnp.concatenate([mixed_top, mixed_ref[0:16, :].astype(F32)[8:16], mixed_ref[16:, :].astype(F32)], axis=0)
    key_out[...] = (gated_grad * mixed).astype(BF)
    mixed_grad = (gated_grad * key_ref[...].astype(F32)).astype(BF)
    mixed_out[...] = mixed_grad
    mixed_grad = mixed_grad.astype(F32)
    mixed_top_out[...] = mixed_grad[0:8].astype(BF)
    wide_ref[0:8, :] = got_top
    wide_ref[8:, :] = value_ref[...].astype(F32)
    sums = []
    for lag in range(short_len):
        sums.append(jnp.sum(mixed_grad * wide_ref[8 - lag : 8 - lag + ROWS, :], axis=0, keepdims=True))
    short_sum = jnp.concatenate(sums + [jnp.zeros((16 - short_len, width), F32)], axis=0)
    for block in range(width // 128):
        lanes = slice(block * 128, block * 128 + 128)
        part_ref[block, 0:ROWS, :] = long_sum[:, lanes].astype(part_ref.dtype)
        part_ref[block, ROWS : ROWS + 16, :] = short_sum[:, lanes].astype(part_ref.dtype)


def rest_kernel(
    up_ref, got_ref, gated_top_ref, before_ref, grad_ref, mixed_ref, rim_ref, short_ref, long_ref,
    hi_ref, lo_ref, near_ref, inv_ref, query_out, value_out, wide_ref,
):
    gated = with_heads(gated_top_ref[...].astype(F32), up_ref, before_ref[...].astype(F32), got_ref)
    gated_spec = dot(hi_ref[...], gated) + dot(lo_ref[...], gated)
    taps_spec = dot(near_ref[...], twice(long_ref[...]))
    long_out = inverse(inv_ref, product(gated_spec, taps_spec, False))
    query_out[...] = (grad_ref[...].astype(F32) * long_out).astype(BF)
    wide_ref[0:ROWS, :] = mixed_ref[...].astype(F32)
    wide_ref[ROWS:, :] = rim_ref[...].astype(F32)
    total = short_ref[0:1, :] * wide_ref[0:ROWS, :]
    for lag in range(1, short_ref.shape[0]):
        total = total + short_ref[lag : lag + 1, :] * wide_ref[lag : lag + ROWS, :]
    value_out[...] = total.astype(BF)


def line_kernel(arrived_ref, spread_ref):
    total = arrived_ref[0].astype(F32)
    for device in range(1, arrived_ref.shape[0]):
        total = total + arrived_ref[device].astype(F32)
    message = total.astype(BF)
    for device in range(spread_ref.shape[0]):
        spread_ref[device] = message


def piece_kernel(arrived_ref, spread_ref):
    total = arrived_ref[0].astype(F32)
    for device in range(1, arrived_ref.shape[0]):
        total = total + arrived_ref[device].astype(F32)
    square = jnp.sum(jnp.sum(total * total, axis=1, keepdims=True), axis=0, keepdims=True)
    high = square.astype(BF).astype(F32)
    row = lax.broadcasted_iota(jnp.int32, (8, 128), 0)
    norm_rows = jnp.where(row == 0, high, jnp.where(row == 1, square - high, 0.0))
    message = jnp.concatenate([total[: ROWS + 8], norm_rows], axis=0).astype(BF)
    for device in range(spread_ref.shape[0]):
        spread_ref[device] = message


def norm_kernel(pieces_ref, norm_ref):
    total = pieces_ref[0, ROWS:, :].astype(F32)
    for piece in range(1, pieces_ref.shape[0]):
        total = total + pieces_ref[piece, ROWS:, :].astype(F32)
    square = total[8:9] + total[9:10]
    norm_ref[...] = jnp.broadcast_to(square[None], norm_ref.shape)


def scale_kernel(limit, core_ref, mine_ref, other_ref, norms_ref, long_ref, short_ref):
    norm_sq = norms_ref[0]
    for device in range(1, norms_ref.shape[0]):
        norm_sq = norm_sq + norms_ref[device]
    factor = limit / jnp.sqrt(norm_sq + 1e-06)
    short_len = short_ref.shape[0]

    def write(pieces_ref):
        for block in range(pieces_ref.shape[0]):
            lanes = slice(block * 128, block * 128 + 128)
            piece = pieces_ref[block].astype(F32) * factor
            long_ref[:, lanes] = piece[:ROWS].astype(BF)
            short_ref[:, lanes] = piece[ROWS : ROWS + short_len].astype(BF)

    @pl.when(pl.program_id(0) == 0)
    def _():
        write(mine_ref)

    @pl.when(pl.program_id(0) == 1)
    def _():
        write(other_ref)


def params(limit=VMEM):
    return pltpu.CompilerParams(vmem_limit_bytes=limit)


def shifted(value, by):
    devices = lax.axis_size("ctx")
    return lax.ppermute(value, "ctx", [(i, i + by) for i in range(devices) if 0 <= i + by < devices])


def on_device(gate_query, gate_key, input_value, out_grad, short_taps, long_taps):
    query_rows, key_rows, value_rows, grad_rows = gate_query[0], gate_key[0], input_value[0], out_grad[0]
    chan_width = query_rows.shape[1]
    half_width = chan_width // 2
    short_len, long_len = short_taps.shape[0], long_taps.shape[0]
    core = lax.axis_index("dp").astype(jnp.int32).reshape(1)
    devices = lax.axis_size("ctx")
    per_half = half_width // WIDTH
    struct = jax.ShapeDtypeStruct
    count = chan_width // WIDTH

    def chan(rows):
        return pl.BlockSpec((rows, WIDTH), lambda i: (0, i))

    wide = struct((ROWS, chan_width), BF)
    top = struct((8, chan_width), BF)
    up, down, mixed = pl.pallas_call(
        gate_kernel,
        out_shape=(wide, wide, wide),
        grid=(count,),
        in_specs=[chan(ROWS), chan(ROWS), chan(ROWS), chan(ROWS), chan(short_len)],
        out_specs=[chan(ROWS), chan(ROWS), chan(ROWS)],
        scratch_shapes=[pltpu.VMEM((ROWS + 8, WIDTH), F32)],
        compiler_params=params(),
        name="gates",
    )(query_rows, key_rows, value_rows, grad_rows, short_taps)
    got = shifted(up, 1)
    back = shifted(down, -1)

    fwd_hi, fwd_lo, near, away, inv_both = (jnp.asarray(t) for t in tables())

    def run_sums(slot, kept):
        def half(rows):
            return pl.BlockSpec((rows, WIDTH), lambda i, core: (0, half_of(slot, core[0]) * per_half + i))

        table = pl.BlockSpec((256, 256), lambda i, core: (0, 0))
        part = struct((half_width // 128, ROWS + 16, 128), BF if slot == 0 else F32)
        in_specs = [half(ROWS)] * 7 + [half(short_len), half(long_len)] + [table] * 5
        first = 1 + len(in_specs)
        return pl.pallas_call(
            sums_kernel,
            out_shape=(wide, wide, top, top, part),
            grid_spec=pltpu.PrefetchScalarGridSpec(
                num_scalar_prefetch=1,
                grid=(per_half,),
                in_specs=in_specs + [pl.BlockSpec(memory_space=pl.ANY)] * len(kept),
                out_specs=[
                    half(ROWS), half(ROWS), half(8), half(8),
                    pl.BlockSpec((WIDTH // 128, ROWS + 16, 128), lambda i, core: (i, 0, 0)),
                ],
                scratch_shapes=[pltpu.VMEM((ROWS + 8, WIDTH), F32)],
            ),
            input_output_aliases={first + k: k for k in range(len(kept))},
            compiler_params=params(),
            cost_estimate=pl.CostEstimate(flops=2_000_000_000, bytes_accessed=4_000_000, transcendentals=0),
            name=f"sums_{slot}",
        )(
            core, up, got, down, back, mixed, key_rows, value_rows, short_taps, long_taps,
            fwd_hi, fwd_lo, near, away, inv_both, *kept,
        )

    *kept, part_sent = run_sums(0, ())
    part_got = lax.ppermute(part_sent, "dp", [(0, 1), (1, 0)])
    key_grad, mixed_grad, gated_top, mixed_top, part_own = run_sums(1, tuple(kept))

    blocks = half_width // 128
    lines = devices // blocks
    along = [[line * blocks + i for i in range(blocks)] for line in range(lines)]
    across = [[line * blocks + i for line in range(lines)] for i in range(blocks)]
    depth = ROWS + 16

    def swap(value, groups):
        return lax.all_to_all(value, "ctx", 0, 0, tiled=True, axis_index_groups=groups)

    def small_call(kernel, name, count):
        return pl.pallas_call(kernel, out_shape=struct((count, depth, 128), BF), compiler_params=params(SMALL), name=name)

    total = (part_own + part_got.astype(F32)).astype(BF)
    before = shifted(gated_top, 1)
    rim = shifted(mixed_top, -1)
    scattered = small_call(line_kernel, "line", lines)(swap(total, along))
    scattered, before, rim = lax.optimization_barrier((scattered, before, rim))
    spread = small_call(piece_kernel, "piece", blocks)(swap(scattered, across))
    gathered = swap(spread, along)
    table = pl.BlockSpec((256, 256), lambda i: (0, 0))
    query_grad, value_grad = pl.pallas_call(
        rest_kernel,
        out_shape=(wide, wide),
        grid=(count,),
        in_specs=[
            chan(ROWS), chan(ROWS), chan(8), chan(8), chan(ROWS), chan(ROWS), chan(8),
            chan(short_len), chan(long_len), table, table, table, table,
        ],
        out_specs=[chan(ROWS), chan(ROWS)],
        scratch_shapes=[pltpu.VMEM((ROWS + 8, WIDTH), F32)],
        compiler_params=params(),
        cost_estimate=pl.CostEstimate(flops=4_000_000_000, bytes_accessed=5_000_000, transcendentals=0),
        name="rest",
    )(
        up, got, gated_top, before, grad_rows, mixed_grad, rim, short_taps, long_taps,
        fwd_hi, fwd_lo, near, inv_both,
    )

    gathered, query_grad, value_grad = lax.optimization_barrier((gathered, query_grad, value_grad))
    ways = lax.axis_size("tp")
    norms = pl.pallas_call(
        norm_kernel,
        out_shape=struct((2 * ways, 1, 128), F32),
        compiler_params=params(SMALL),
        name="norm",
    )(gathered)
    norms = lax.all_to_all(norms, ("tp", "dp"), 0, 0, tiled=True)
    other = lax.ppermute(gathered, "dp", [(0, 1), (1, 0)])
    limit = math.sqrt((long_len + short_len) * chan_width * ways)
    whole = pl.BlockSpec((blocks, depth, 128), lambda i, core: (0, 0, 0))

    def result(rows):
        return pl.BlockSpec((rows, half_width), lambda i, core: (0, jnp.where(i == 0, core[0], 1 - core[0])))

    long_grad, short_grad = pl.pallas_call(
        functools.partial(scale_kernel, limit),
        out_shape=(struct((long_len, chan_width), BF), struct((short_len, chan_width), BF)),
        grid_spec=pltpu.PrefetchScalarGridSpec(
            num_scalar_prefetch=1,
            grid=(2,),
            in_specs=[whole, whole, pl.BlockSpec((2 * ways, 1, 128), lambda i, core: (0, 0, 0))],
            out_specs=[result(long_len), result(short_len)],
        ),
        compiler_params=params(SMALL),
        name="scale",
    )(core, gathered, other, norms)
    return (query_grad[None], key_grad[None], value_grad[None], long_grad, short_grad)


def solution(mesh):
    split = P("dp", "ctx", "tp")
    taps = P(None, "tp")
    return jax.shard_map(
        on_device,
        mesh=mesh,
        in_specs=(split, split, split, split, taps, taps),
        out_specs=(split, split, split, taps, taps),
        check_vma=False,
    )
```

```python
import functools
import math

import jax
import jax.numpy as jnp
import numpy as np
from jax import lax
from jax.experimental import pallas as pl
from jax.experimental.pallas import tpu as pltpu
from jax.sharding import PartitionSpec as P

BF = jnp.bfloat16
F32 = jnp.float32
ROWS = 128
WIDTH = 512
VMEM = 60 * 1024 * 1024
SMALL = 16 * 1024 * 1024


def split_table(table):
    high = table.astype(np.float32).astype(jnp.bfloat16)
    low = (table - high.astype(np.float64)).astype(np.float32).astype(jnp.bfloat16)
    return high, low


def tables():
    freq = np.arange(128)[:, None]
    place = np.arange(256)[None, :]
    angle = (freq * place % 256) * (2.0 * np.pi / 256)
    fwd = np.concatenate([np.cos(angle), -np.sin(angle)], axis=0)
    fwd[128] = 1.0 - 2.0 * (np.arange(256) % 2)
    weight = np.full((256,), 2.0 / 256)
    weight[0] = weight[128] = 1.0 / 256
    inv = (fwd * weight[:, None]).T
    fwd_hi, fwd_lo = split_table(fwd)
    inv_hi, inv_lo = split_table(inv)
    near = np.concatenate([fwd_hi[:, :128], fwd_lo[:, :128]], axis=1)
    away = np.concatenate([fwd_hi[:, 128:], fwd_lo[:, 128:]], axis=1)
    inv_both = np.concatenate([inv_hi[:ROWS], inv_lo[:ROWS]], axis=0)
    return fwd_hi, fwd_lo, near, away, inv_both


def half_of(slot, core):
    return jnp.where(core == 0, 1 - slot, slot)


def gate_kernel(core_ref, query_ref, key_ref, value_ref, grad_ref, taps_ref, up_ref, down_ref, mixed_ref, wide_ref):
    short_len = taps_ref.shape[0]
    width = wide_ref.shape[1]
    down_ref[...] = (grad_ref[...].astype(F32) * query_ref[...].astype(F32)).astype(BF)
    wide_ref[0:8, :] = jnp.zeros((8, width), F32)
    wide_ref[8:, :] = value_ref[...].astype(F32)
    total = taps_ref[0:1, :] * wide_ref[8 : 8 + ROWS, :]
    for lag in range(1, short_len):
        total = total + taps_ref[lag : lag + 1, :] * wide_ref[8 - lag : 8 - lag + ROWS, :]
    mixed = total.astype(BF)
    mixed_ref[...] = mixed
    gated = key_ref[...].astype(F32) * mixed.astype(F32)
    row = lax.broadcasted_iota(jnp.int32, (8, width), 0)
    wide_ref[0:16, :] = gated[0:16]
    top = jnp.where(row < 2, wide_ref[6:14, :], wide_ref[ROWS : ROWS + 8, :])
    up_ref[0:16, :] = jnp.concatenate([top, gated[8:16]], axis=0).astype(BF)
    up_ref[16:ROWS, :] = gated[16:].astype(BF)


def own_head(wide_ref, tail, key_ref, value_ref, taps_ref):
    value = value_ref[0:16, :].astype(F32)[0:8]
    key = key_ref[0:16, :].astype(F32)[0:8]
    wide_ref[0:8, :] = tail
    wide_ref[8:16, :] = value
    total = taps_ref[0:1, :] * value
    for lag in range(1, taps_ref.shape[0]):
        total = total + taps_ref[lag : lag + 1, :] * wide_ref[8 - lag : 16 - lag, :]
    mixed = total.astype(BF).astype(F32)
    return mixed, (key * mixed).astype(BF).astype(F32)


def with_heads(own_head_rows, up_ref, got_head_rows, got_ref):
    parts = []
    for head, ref in ((own_head_rows, up_ref), (got_head_rows, got_ref)):
        parts.append(jnp.concatenate([head, ref[0:16, :].astype(F32)[8:16]], axis=0).astype(BF))
        parts.append(ref[16:ROWS, :])
    return jnp.concatenate(parts, axis=0)


def dot(left, right):
    return jnp.dot(left, right, preferred_element_type=F32)


def product(first, second, conjugate):
    first_re, first_im = first[:128], first[128:]
    second_re, second_im = second[:128], second[128:]
    edge = lax.broadcasted_iota(jnp.int32, first_re.shape, 0) == 0
    cross = first_im * second_im
    inner = jnp.where(edge, 0.0, cross)
    if conjugate:
        real = first_re * second_re + inner
        imag = first_im * second_re - first_re * second_im
    else:
        real = first_re * second_re - inner
        imag = first_re * second_im + first_im * second_re
    return jnp.concatenate([real, jnp.where(edge, cross, imag)], axis=0)


def inverse(inv_ref, spec):
    high = spec.astype(BF)
    low = (spec - high.astype(F32)).astype(BF)
    both = dot(inv_ref[...], high)
    return both[:ROWS] + both[ROWS:] + dot(inv_ref[0:ROWS, :], low)


def twice(rows):
    return jnp.concatenate([rows, rows], axis=0)


def sums_kernel(
    core_ref, up_ref, got_ref, down_ref, back_ref, mixed_ref, key_ref, value_ref, short_ref, long_ref,
    hi_ref, lo_ref, near_ref, away_ref, inv_ref, *rest,
):
    key_out, mixed_out, gated_top_out, mixed_top_out, part_ref, wide_ref = rest[-6:]
    short_len = short_ref.shape[0]
    width = wide_ref.shape[1]
    row = lax.broadcasted_iota(jnp.int32, (8, width), 0)
    got_top = got_ref[0:16, :].astype(F32)[0:8]
    mixed_top, gated_top = own_head(wide_ref, got_top, key_ref, value_ref, short_ref)
    gated_top_out[...] = gated_top.astype(BF)
    wide_ref[8:16, :] = got_top
    before = jnp.where(row < 6, 0.0, wide_ref[2:10, :])
    gated = with_heads(gated_top, up_ref, before, got_ref)
    mid = down_ref[...]
    ahead = back_ref[...]
    gated_spec = dot(hi_ref[...], gated) + dot(lo_ref[...], gated)
    mid_spec = dot(near_ref[...], twice(mid))
    both_spec = mid_spec + dot(away_ref[...], twice(ahead))
    taps_spec = dot(near_ref[...], twice(long_ref[...]))
    long_sum = inverse(inv_ref, product(mid_spec, gated_spec, True))
    gated_grad = inverse(inv_ref, product(both_spec, taps_spec, True))
    next_top = back_ref[0:16, :].astype(F32)[0:8]
    lines = [jnp.zeros((3, width), F32)]
    for gap in range(5, 0, -1):
        line = gated_top[gap : gap + 1] * next_top[0:1]
        for r in range(gap + 1, 6):
            line = line + gated_top[r : r + 1] * next_top[r - gap : r - gap + 1]
        lines.append(line)
    long_end = long_sum[ROWS - 8 :] + jnp.concatenate(lines, axis=0)
    long_sum = jnp.concatenate([long_sum[: ROWS - 8], long_end], axis=0)
    mixed = jnp.concatenate([mixed_top, mixed_ref[0:16, :].astype(F32)[8:16], mixed_ref[16:, :].astype(F32)], axis=0)
    key_out[...] = (gated_grad * mixed).astype(BF)
    mixed_grad = (gated_grad * key_ref[...].astype(F32)).astype(BF)
    mixed_out[...] = mixed_grad
    mixed_grad = mixed_grad.astype(F32)
    mixed_top_out[...] = mixed_grad[0:8].astype(BF)
    wide_ref[0:8, :] = got_top
    wide_ref[8:, :] = value_ref[...].astype(F32)
    sums = []
    for lag in range(short_len):
        sums.append(jnp.sum(mixed_grad * wide_ref[8 - lag : 8 - lag + ROWS, :], axis=0, keepdims=True))
    short_sum = jnp.concatenate(sums + [jnp.zeros((16 - short_len, width), F32)], axis=0)
    for block in range(width // 128):
        lanes = slice(block * 128, block * 128 + 128)
        part_ref[block, 0:ROWS, :] = long_sum[:, lanes].astype(part_ref.dtype)
        part_ref[block, ROWS : ROWS + 16, :] = short_sum[:, lanes].astype(part_ref.dtype)


def rest_kernel(
    core_ref, up_ref, got_ref, gated_top_ref, before_ref, grad_ref, mixed_ref, rim_ref, short_ref, long_ref,
    hi_ref, lo_ref, near_ref, inv_ref, *rest,
):
    query_out, value_out, wide_ref = rest[-3:]
    gated = with_heads(gated_top_ref[...].astype(F32), up_ref, before_ref[...].astype(F32), got_ref)
    gated_spec = dot(hi_ref[...], gated) + dot(lo_ref[...], gated)
    taps_spec = dot(near_ref[...], twice(long_ref[...]))
    long_out = inverse(inv_ref, product(gated_spec, taps_spec, False))
    query_out[...] = (grad_ref[...].astype(F32) * long_out).astype(BF)
    wide_ref[0:ROWS, :] = mixed_ref[...].astype(F32)
    wide_ref[ROWS:, :] = rim_ref[...].astype(F32)
    total = short_ref[0:1, :] * wide_ref[0:ROWS, :]
    for lag in range(1, short_ref.shape[0]):
        total = total + short_ref[lag : lag + 1, :] * wide_ref[lag : lag + ROWS, :]
    value_out[...] = total.astype(BF)


def line_kernel(arrived_ref, spread_ref):
    total = arrived_ref[0].astype(F32)
    for device in range(1, arrived_ref.shape[0]):
        total = total + arrived_ref[device].astype(F32)
    message = total.astype(BF)
    for device in range(spread_ref.shape[0]):
        spread_ref[device] = message


def piece_kernel(arrived_ref, spread_ref):
    total = arrived_ref[0].astype(F32)
    for device in range(1, arrived_ref.shape[0]):
        total = total + arrived_ref[device].astype(F32)
    square = jnp.sum(jnp.sum(total * total, axis=1, keepdims=True), axis=0, keepdims=True)
    high = square.astype(BF).astype(F32)
    row = lax.broadcasted_iota(jnp.int32, (8, 128), 0)
    norm_rows = jnp.where(row == 0, high, jnp.where(row == 1, square - high, 0.0))
    message = jnp.concatenate([total[: ROWS + 8], norm_rows], axis=0).astype(BF)
    for device in range(spread_ref.shape[0]):
        spread_ref[device] = message


def norm_kernel(pieces_ref, norm_ref):
    total = pieces_ref[0, ROWS:, :].astype(F32)
    for piece in range(1, pieces_ref.shape[0]):
        total = total + pieces_ref[piece, ROWS:, :].astype(F32)
    square = total[8:9] + total[9:10]
    norm_ref[...] = jnp.broadcast_to(square[None], norm_ref.shape)


def scale_kernel(limit, core_ref, mine_ref, other_ref, norms_ref, long_ref, short_ref):
    norm_sq = norms_ref[0]
    for device in range(1, norms_ref.shape[0]):
        norm_sq = norm_sq + norms_ref[device]
    factor = limit / jnp.sqrt(norm_sq + 1e-06)
    short_len = short_ref.shape[0]

    def write(pieces_ref):
        for block in range(pieces_ref.shape[0]):
            lanes = slice(block * 128, block * 128 + 128)
            piece = pieces_ref[block].astype(F32) * factor
            long_ref[:, lanes] = piece[:ROWS].astype(BF)
            short_ref[:, lanes] = piece[ROWS : ROWS + short_len].astype(BF)

    @pl.when(pl.program_id(0) == 0)
    def _():
        write(mine_ref)

    @pl.when(pl.program_id(0) == 1)
    def _():
        write(other_ref)


def params(limit=VMEM):
    return pltpu.CompilerParams(vmem_limit_bytes=limit)


def shifted(value, by):
    devices = lax.axis_size("ctx")
    return lax.ppermute(value, "ctx", [(i, i + by) for i in range(devices) if 0 <= i + by < devices])


def on_device(gate_query, gate_key, input_value, out_grad, short_taps, long_taps):
    query_rows, key_rows, value_rows, grad_rows = gate_query[0], gate_key[0], input_value[0], out_grad[0]
    chan_width = query_rows.shape[1]
    half_width = chan_width // 2
    short_len, long_len = short_taps.shape[0], long_taps.shape[0]
    core = lax.axis_index("dp").astype(jnp.int32).reshape(1)
    devices = lax.axis_size("ctx")
    per_half = half_width // WIDTH
    struct = jax.ShapeDtypeStruct
    def half(slot):
        return lambda rows: pl.BlockSpec((rows, WIDTH), lambda i, core: (0, half_of(slot, core[0]) * per_half + i))

    def held(rows):
        return pl.BlockSpec((rows, WIDTH), lambda i, core: (0, i))

    def call(kernel, name, slot, operands, specs, kept, out_shape, out_specs, cost):
        first = 1 + len(specs)
        return pl.pallas_call(
            kernel,
            out_shape=out_shape,
            grid_spec=pltpu.PrefetchScalarGridSpec(
                num_scalar_prefetch=1,
                grid=(per_half,),
                in_specs=specs + [pl.BlockSpec(memory_space=pl.ANY)] * len(kept),
                out_specs=out_specs,
                scratch_shapes=[pltpu.VMEM((ROWS + 8, WIDTH), F32)],
            ),
            input_output_aliases={first + k: k for k in range(len(kept))},
            compiler_params=params(),
            cost_estimate=cost,
            name=f"{name}_{slot}",
        )(core, *operands, *kept)

    little = pl.CostEstimate(flops=1000, bytes_accessed=1000, transcendentals=0)
    wide = struct((ROWS, chan_width), BF)
    top = struct((8, chan_width), BF)
    own = struct((ROWS, half_width), BF)
    ups, downs, mixeds, gots, backs = [], [], [], [], []
    for slot in range(2):
        part = half(slot)
        up, down, mixed = call(
            gate_kernel, "gates", slot, (query_rows, key_rows, value_rows, grad_rows, short_taps),
            [part(ROWS), part(ROWS), part(ROWS), part(ROWS), part(short_len)], (),
            (own, own, own), [held(ROWS)] * 3, little,
        )
        ups.append(up)
        downs.append(down)
        mixeds.append(mixed)
        gots.append(shifted(up, 1))
        backs.append(shifted(down, -1))

    ups[0], ups[1], downs[1] = lax.optimization_barrier((ups[0], ups[1], downs[1]))

    fwd_hi, fwd_lo, near, away, inv_both = (jnp.asarray(t) for t in tables())
    table = pl.BlockSpec((256, 256), lambda i, core: (0, 0))

    def run_sums(slot, kept):
        part = half(slot)
        return call(
            sums_kernel, "sums", slot,
            (
                ups[slot], gots[slot], downs[slot], backs[slot], mixeds[slot], key_rows, value_rows, short_taps, long_taps,
                fwd_hi, fwd_lo, near, away, inv_both,
            ),
            [held(ROWS)] * 5 + [part(ROWS), part(ROWS), part(short_len), part(long_len)] + [table] * 5,
            kept,
            (wide, wide, top, top, struct((half_width // 128, ROWS + 16, 128), BF if slot == 0 else F32)),
            [part(ROWS), part(ROWS), part(8), part(8), pl.BlockSpec((WIDTH // 128, ROWS + 16, 128), lambda i, core: (i, 0, 0))],
            pl.CostEstimate(flops=6_000_000_000, bytes_accessed=8_000_000, transcendentals=0),
        )

    def run_rest(slot, kept, before, rim):
        part = half(slot)
        return call(
            rest_kernel, "rest", slot,
            (
                ups[slot], gots[slot], gated_top, before, grad_rows, mixed_grad, rim, short_taps, long_taps,
                fwd_hi, fwd_lo, near, inv_both,
            ),
            [held(ROWS), held(ROWS), part(8), part(8), part(ROWS), part(ROWS), part(8), part(short_len), part(long_len)]
            + [table] * 4,
            kept,
            (wide, wide),
            [part(ROWS), part(ROWS)],
            pl.CostEstimate(flops=4_000_000_000, bytes_accessed=5_000_000, transcendentals=0),
        )

    *kept, part_sent = run_sums(0, ())
    part_got = lax.ppermute(part_sent, "dp", [(0, 1), (1, 0)])
    key_grad, mixed_grad, gated_top, mixed_top, part_own = run_sums(1, tuple(kept))

    blocks = half_width // 128
    lines = devices // blocks
    along = [[line * blocks + i for i in range(blocks)] for line in range(lines)]
    across = [[line * blocks + i for line in range(lines)] for i in range(blocks)]
    depth = ROWS + 16

    def swap(value, groups):
        return lax.all_to_all(value, "ctx", 0, 0, tiled=True, axis_index_groups=groups)

    def small_call(kernel, name, count):
        return pl.pallas_call(kernel, out_shape=struct((count, depth, 128), BF), compiler_params=params(SMALL), name=name)

    total = (part_own + part_got.astype(F32)).astype(BF)
    scattered = swap(total, along)
    scattered, gated_top, mixed_top = lax.optimization_barrier((scattered, gated_top, mixed_top))
    before = shifted(gated_top, 1)
    rim = shifted(mixed_top, -1)
    crossed = swap(small_call(line_kernel, "line", lines)(scattered), across)
    crossed, before, rim = lax.optimization_barrier((crossed, before, rim))
    gathered = swap(small_call(piece_kernel, "piece", blocks)(crossed), along)
    grads = run_rest(1, run_rest(0, (), before, rim), before, rim)
    gathered, query_grad, value_grad = lax.optimization_barrier((gathered, *grads))
    ways = lax.axis_size("tp")
    norms = pl.pallas_call(
        norm_kernel,
        out_shape=struct((2 * ways, 1, 128), F32),
        compiler_params=params(SMALL),
        name="norm",
    )(gathered)
    norms = lax.all_to_all(norms, ("tp", "dp"), 0, 0, tiled=True)
    other = lax.ppermute(gathered, "dp", [(0, 1), (1, 0)])
    limit = math.sqrt((long_len + short_len) * chan_width * ways)
    whole = pl.BlockSpec((blocks, depth, 128), lambda i, core: (0, 0, 0))

    def result(rows):
        return pl.BlockSpec((rows, half_width), lambda i, core: (0, jnp.where(i == 0, core[0], 1 - core[0])))

    long_grad, short_grad = pl.pallas_call(
        functools.partial(scale_kernel, limit),
        out_shape=(struct((long_len, chan_width), BF), struct((short_len, chan_width), BF)),
        grid_spec=pltpu.PrefetchScalarGridSpec(
            num_scalar_prefetch=1,
            grid=(2,),
            in_specs=[whole, whole, pl.BlockSpec((2 * ways, 1, 128), lambda i, core: (0, 0, 0))],
            out_specs=[result(long_len), result(short_len)],
        ),
        compiler_params=params(SMALL),
        name="scale",
    )(core, gathered, other, norms)
    return (query_grad[None], key_grad[None], value_grad[None], long_grad, short_grad)


def solution(mesh):
    split = P("dp", "ctx", "tp")
    taps = P(None, "tp")
    return jax.shard_map(
        on_device,
        mesh=mesh,
        in_specs=(split, split, split, split, taps, taps),
        out_specs=(split, split, split, taps, taps),
        check_vma=False,
    )
```

```python
import functools
import math

import jax
import jax.numpy as jnp
import numpy as np
from jax import lax
from jax.experimental import pallas as pl
from jax.experimental.pallas import tpu as pltpu
from jax.sharding import PartitionSpec as P

BF = jnp.bfloat16
F32 = jnp.float32
ROWS = 128
WIDTH = 512
VMEM = 60 * 1024 * 1024
SMALL = 16 * 1024 * 1024


def split_table(table):
    high = table.astype(np.float32).astype(jnp.bfloat16)
    low = (table - high.astype(np.float64)).astype(np.float32).astype(jnp.bfloat16)
    return high, low


def tables():
    freq = np.arange(128)[:, None]
    place = np.arange(256)[None, :]
    angle = (freq * place % 256) * (2.0 * np.pi / 256)
    fwd = np.concatenate([np.cos(angle), -np.sin(angle)], axis=0)
    fwd[128] = 1.0 - 2.0 * (np.arange(256) % 2)
    weight = np.full((256,), 2.0 / 256)
    weight[0] = weight[128] = 1.0 / 256
    inv = (fwd * weight[:, None]).T
    fwd_hi, fwd_lo = split_table(fwd)
    inv_hi, inv_lo = split_table(inv)
    near = np.concatenate([fwd_hi[:, :128], fwd_lo[:, :128]], axis=1)
    away = np.concatenate([fwd_hi[:, 128:], fwd_lo[:, 128:]], axis=1)
    inv_both = np.concatenate([inv_hi[:ROWS], inv_lo[:ROWS]], axis=0)
    return fwd_hi, fwd_lo, near, away, inv_both


def half_of(slot, core):
    return jnp.where(core == 0, 1 - slot, slot)


def gate_kernel(place_ref, query_ref, key_ref, value_ref, grad_ref, taps_ref, first_ref, second_ref, mixed_ref, wide_ref):
    short_len = taps_ref.shape[0]
    width = wide_ref.shape[1]
    mid = (grad_ref[...].astype(F32) * query_ref[...].astype(F32)).astype(BF)
    wide_ref[0:8, :] = jnp.zeros((8, width), F32)
    wide_ref[8:, :] = value_ref[...].astype(F32)
    total = taps_ref[0:1, :] * wide_ref[8 : 8 + ROWS, :]
    for lag in range(1, short_len):
        total = total + taps_ref[lag : lag + 1, :] * wide_ref[8 - lag : 8 - lag + ROWS, :]
    mixed = total.astype(BF)
    mixed_ref[...] = mixed
    gated = key_ref[...].astype(F32) * mixed.astype(F32)
    row = lax.broadcasted_iota(jnp.int32, (8, width), 0)
    wide_ref[0:16, :] = gated[0:16]
    top = jnp.where(row < 2, wide_ref[6:14, :], wide_ref[ROWS : ROWS + 8, :])
    begin = jnp.concatenate([top, gated[8:16]], axis=0).astype(BF)
    gated = gated[16:].astype(BF)

    def write(up_ref, down_ref):
        up_ref[0:16, :] = begin
        up_ref[16:ROWS, :] = gated
        down_ref[...] = mid

    @pl.when(place_ref[1] == 1)
    def _():
        write(first_ref, second_ref)

    @pl.when(place_ref[1] == 0)
    def _():
        write(second_ref, first_ref)


def own_head(wide_ref, tail, key_ref, value_ref, taps_ref):
    value = value_ref[0:16, :].astype(F32)[0:8]
    key = key_ref[0:16, :].astype(F32)[0:8]
    wide_ref[0:8, :] = tail
    wide_ref[8:16, :] = value
    total = taps_ref[0:1, :] * value
    for lag in range(1, taps_ref.shape[0]):
        total = total + taps_ref[lag : lag + 1, :] * wide_ref[8 - lag : 16 - lag, :]
    mixed = total.astype(BF).astype(F32)
    return mixed, (key * mixed).astype(BF).astype(F32)


def by_direction(place_ref, first_ref, second_ref):
    odd = place_ref[1] == 1
    first, second = first_ref[...], second_ref[...]
    return jnp.where(odd, first, second), jnp.where(odd, second, first)


def with_heads(own_head_rows, up, got_head_rows, got):
    parts = []
    for head, rows in ((own_head_rows, up), (got_head_rows, got)):
        parts.append(jnp.concatenate([head, rows[0:16].astype(F32)[8:16]], axis=0).astype(BF))
        parts.append(rows[16:])
    return jnp.concatenate(parts, axis=0)


def dot(left, right):
    return jnp.dot(left, right, preferred_element_type=F32)


def product(first, second, conjugate):
    first_re, first_im = first[:128], first[128:]
    second_re, second_im = second[:128], second[128:]
    edge = lax.broadcasted_iota(jnp.int32, first_re.shape, 0) == 0
    cross = first_im * second_im
    inner = jnp.where(edge, 0.0, cross)
    if conjugate:
        real = first_re * second_re + inner
        imag = first_im * second_re - first_re * second_im
    else:
        real = first_re * second_re - inner
        imag = first_re * second_im + first_im * second_re
    return jnp.concatenate([real, jnp.where(edge, cross, imag)], axis=0)


def inverse(inv_ref, spec):
    high = spec.astype(BF)
    low = (spec - high.astype(F32)).astype(BF)
    both = dot(inv_ref[...], high)
    return both[:ROWS] + both[ROWS:] + dot(inv_ref[0:ROWS, :], low)


def twice(rows):
    return jnp.concatenate([rows, rows], axis=0)


def sums_kernel(
    place_ref, sent_a_ref, sent_b_ref, got_a_ref, got_b_ref, mixed_ref, key_ref, value_ref, short_ref, long_ref,
    hi_ref, lo_ref, near_ref, away_ref, inv_ref, *rest,
):
    key_out, mixed_out, gated_top_out, mixed_top_out, part_ref, wide_ref = rest[-6:]
    short_len = short_ref.shape[0]
    width = wide_ref.shape[1]
    row = lax.broadcasted_iota(jnp.int32, (8, width), 0)
    up, mid = by_direction(place_ref, sent_a_ref, sent_b_ref)
    ahead, got = by_direction(place_ref, got_a_ref, got_b_ref)
    got_top = got[0:16].astype(F32)[0:8]
    mixed_top, gated_top = own_head(wide_ref, got_top, key_ref, value_ref, short_ref)
    gated_top_out[...] = gated_top.astype(BF)
    wide_ref[8:16, :] = got_top
    before = jnp.where(row < 6, 0.0, wide_ref[2:10, :])
    gated = with_heads(gated_top, up, before, got)
    gated_spec = dot(hi_ref[...], gated) + dot(lo_ref[...], gated)
    mid_spec = dot(near_ref[...], twice(mid))
    both_spec = mid_spec + dot(away_ref[...], twice(ahead))
    taps_spec = dot(near_ref[...], twice(long_ref[...]))
    long_sum = inverse(inv_ref, product(mid_spec, gated_spec, True))
    gated_grad = inverse(inv_ref, product(both_spec, taps_spec, True))
    next_top = ahead[0:16].astype(F32)[0:8]
    lines = [jnp.zeros((3, width), F32)]
    for gap in range(5, 0, -1):
        line = gated_top[gap : gap + 1] * next_top[0:1]
        for r in range(gap + 1, 6):
            line = line + gated_top[r : r + 1] * next_top[r - gap : r - gap + 1]
        lines.append(line)
    long_end = long_sum[ROWS - 8 :] + jnp.concatenate(lines, axis=0)
    long_sum = jnp.concatenate([long_sum[: ROWS - 8], long_end], axis=0)
    mixed = jnp.concatenate([mixed_top, mixed_ref[0:16, :].astype(F32)[8:16], mixed_ref[16:, :].astype(F32)], axis=0)
    key_out[...] = (gated_grad * mixed).astype(BF)
    mixed_grad = (gated_grad * key_ref[...].astype(F32)).astype(BF)
    mixed_out[...] = mixed_grad
    mixed_grad = mixed_grad.astype(F32)
    mixed_top_out[...] = mixed_grad[0:8].astype(BF)
    wide_ref[0:8, :] = got_top
    wide_ref[8:, :] = value_ref[...].astype(F32)
    sums = []
    for lag in range(short_len):
        sums.append(jnp.sum(mixed_grad * wide_ref[8 - lag : 8 - lag + ROWS, :], axis=0, keepdims=True))
    short_sum = jnp.concatenate(sums + [jnp.zeros((16 - short_len, width), F32)], axis=0)
    for block in range(width // 128):
        lanes = slice(block * 128, block * 128 + 128)
        part_ref[block, 0:ROWS, :] = long_sum[:, lanes].astype(part_ref.dtype)
        part_ref[block, ROWS : ROWS + 16, :] = short_sum[:, lanes].astype(part_ref.dtype)


def rest_kernel(
    place_ref, sent_a_ref, sent_b_ref, got_a_ref, got_b_ref, gated_top_ref, before_ref, grad_ref, mixed_ref, rim_ref, short_ref, long_ref,
    hi_ref, lo_ref, near_ref, inv_ref, *rest,
):
    query_out, value_out, wide_ref = rest[-3:]
    up, _ = by_direction(place_ref, sent_a_ref, sent_b_ref)
    _, got = by_direction(place_ref, got_a_ref, got_b_ref)
    gated = with_heads(gated_top_ref[...].astype(F32), up, before_ref[...].astype(F32), got)
    gated_spec = dot(hi_ref[...], gated) + dot(lo_ref[...], gated)
    taps_spec = dot(near_ref[...], twice(long_ref[...]))
    long_out = inverse(inv_ref, product(gated_spec, taps_spec, False))
    query_out[...] = (grad_ref[...].astype(F32) * long_out).astype(BF)
    wide_ref[0:ROWS, :] = mixed_ref[...].astype(F32)
    wide_ref[ROWS:, :] = rim_ref[...].astype(F32)
    total = short_ref[0:1, :] * wide_ref[0:ROWS, :]
    for lag in range(1, short_ref.shape[0]):
        total = total + short_ref[lag : lag + 1, :] * wide_ref[lag : lag + ROWS, :]
    value_out[...] = total.astype(BF)


def line_kernel(arrived_ref, spread_ref):
    total = arrived_ref[0].astype(F32)
    for device in range(1, arrived_ref.shape[0]):
        total = total + arrived_ref[device].astype(F32)
    message = total.astype(BF)
    for device in range(spread_ref.shape[0]):
        spread_ref[device] = message


def piece_kernel(arrived_ref, spread_ref):
    total = arrived_ref[0].astype(F32)
    for device in range(1, arrived_ref.shape[0]):
        total = total + arrived_ref[device].astype(F32)
    square = jnp.sum(jnp.sum(total * total, axis=1, keepdims=True), axis=0, keepdims=True)
    high = square.astype(BF).astype(F32)
    row = lax.broadcasted_iota(jnp.int32, (8, 128), 0)
    norm_rows = jnp.where(row == 0, high, jnp.where(row == 1, square - high, 0.0))
    message = jnp.concatenate([total[: ROWS + 8], norm_rows], axis=0).astype(BF)
    for device in range(spread_ref.shape[0]):
        spread_ref[device] = message


def norm_kernel(pieces_ref, norm_ref):
    total = pieces_ref[0, ROWS:, :].astype(F32)
    for piece in range(1, pieces_ref.shape[0]):
        total = total + pieces_ref[piece, ROWS:, :].astype(F32)
    square = total[8:9] + total[9:10]
    norm_ref[...] = jnp.broadcast_to(square[None], norm_ref.shape)


def scale_kernel(limit, place_ref, mine_ref, other_ref, norms_ref, long_ref, short_ref):
    norm_sq = norms_ref[0]
    for device in range(1, norms_ref.shape[0]):
        norm_sq = norm_sq + norms_ref[device]
    factor = limit / jnp.sqrt(norm_sq + 1e-06)
    short_len = short_ref.shape[0]

    def write(pieces_ref):
        for block in range(pieces_ref.shape[0]):
            lanes = slice(block * 128, block * 128 + 128)
            piece = pieces_ref[block].astype(F32) * factor
            long_ref[:, lanes] = piece[:ROWS].astype(BF)
            short_ref[:, lanes] = piece[ROWS : ROWS + short_len].astype(BF)

    @pl.when(pl.program_id(0) == 0)
    def _():
        write(mine_ref)

    @pl.when(pl.program_id(0) == 1)
    def _():
        write(other_ref)


def params(limit=VMEM):
    return pltpu.CompilerParams(vmem_limit_bytes=limit)


def swapped(value, phase):
    devices = lax.axis_size("ctx")
    starts = range(1 - phase, devices - 1, 2)
    return lax.ppermute(value, "ctx", [(i, i + 1) for i in starts] + [(i + 1, i) for i in starts])


def shifted(value, by):
    devices = lax.axis_size("ctx")
    return lax.ppermute(value, "ctx", [(i, i + by) for i in range(devices) if 0 <= i + by < devices])


def on_device(gate_query, gate_key, input_value, out_grad, short_taps, long_taps):
    query_rows, key_rows, value_rows, grad_rows = gate_query[0], gate_key[0], input_value[0], out_grad[0]
    chan_width = query_rows.shape[1]
    half_width = chan_width // 2
    short_len, long_len = short_taps.shape[0], long_taps.shape[0]
    core = jnp.stack([lax.axis_index("dp"), lax.axis_index("ctx") % 2]).astype(jnp.int32)
    devices = lax.axis_size("ctx")
    per_half = half_width // WIDTH
    struct = jax.ShapeDtypeStruct
    def half(slot):
        return lambda rows: pl.BlockSpec((rows, WIDTH), lambda i, core: (0, half_of(slot, core[0]) * per_half + i))

    def held(rows):
        return pl.BlockSpec((rows, WIDTH), lambda i, core: (0, i))

    def call(kernel, name, slot, operands, specs, kept, out_shape, out_specs, cost):
        first = 1 + len(specs)
        return pl.pallas_call(
            kernel,
            out_shape=out_shape,
            grid_spec=pltpu.PrefetchScalarGridSpec(
                num_scalar_prefetch=1,
                grid=(per_half,),
                in_specs=specs + [pl.BlockSpec(memory_space=pl.ANY)] * len(kept),
                out_specs=out_specs,
                scratch_shapes=[pltpu.VMEM((ROWS + 8, WIDTH), F32)],
            ),
            input_output_aliases={first + k: k for k in range(len(kept))},
            compiler_params=params(),
            cost_estimate=cost,
            name=f"{name}_{slot}",
        )(core, *operands, *kept)

    little = pl.CostEstimate(flops=1000, bytes_accessed=1000, transcendentals=0)
    wide = struct((ROWS, chan_width), BF)
    top = struct((8, chan_width), BF)
    own = struct((ROWS, half_width), BF)
    sent, mixeds, got = [], [], []
    for slot in range(2):
        part = half(slot)
        first, second, mixed = call(
            gate_kernel, "gates", slot, (query_rows, key_rows, value_rows, grad_rows, short_taps),
            [part(ROWS), part(ROWS), part(ROWS), part(ROWS), part(short_len)], (),
            (own, own, own), [held(ROWS)] * 3, little,
        )
        sent.append((first, second))
        mixeds.append(mixed)
        got.append((swapped(first, 0), swapped(second, 1)))
    sent = lax.optimization_barrier(sent)

    fwd_hi, fwd_lo, near, away, inv_both = (jnp.asarray(t) for t in tables())
    table = pl.BlockSpec((256, 256), lambda i, core: (0, 0))

    def run_sums(slot, kept):
        part = half(slot)
        return call(
            sums_kernel, "sums", slot,
            (
                *sent[slot], *got[slot], mixeds[slot], key_rows, value_rows, short_taps, long_taps,
                fwd_hi, fwd_lo, near, away, inv_both,
            ),
            [held(ROWS)] * 5 + [part(ROWS), part(ROWS), part(short_len), part(long_len)] + [table] * 5,
            kept,
            (wide, wide, top, top, struct((half_width // 128, ROWS + 16, 128), BF if slot == 0 else F32)),
            [part(ROWS), part(ROWS), part(8), part(8), pl.BlockSpec((WIDTH // 128, ROWS + 16, 128), lambda i, core: (i, 0, 0))],
            pl.CostEstimate(flops=6_000_000_000, bytes_accessed=8_000_000, transcendentals=0),
        )

    def run_rest(slot, kept, before, rim):
        part = half(slot)
        return call(
            rest_kernel, "rest", slot,
            (
                *sent[slot], *got[slot], gated_top, before, grad_rows, mixed_grad, rim, short_taps, long_taps,
                fwd_hi, fwd_lo, near, inv_both,
            ),
            [held(ROWS)] * 4 + [part(8), part(8), part(ROWS), part(ROWS), part(8), part(short_len), part(long_len)]
            + [table] * 4,
            kept,
            (wide, wide),
            [part(ROWS), part(ROWS)],
            pl.CostEstimate(flops=4_000_000_000, bytes_accessed=5_000_000, transcendentals=0),
        )

    *kept, part_sent = run_sums(0, ())
    part_got = lax.ppermute(part_sent, "dp", [(0, 1), (1, 0)])
    key_grad, mixed_grad, gated_top, mixed_top, part_own = run_sums(1, tuple(kept))

    blocks = half_width // 128
    lines = devices // blocks
    along = [[line * blocks + i for i in range(blocks)] for line in range(lines)]
    across = [[line * blocks + i for line in range(lines)] for i in range(blocks)]
    depth = ROWS + 16

    def swap(value, groups):
        return lax.all_to_all(value, "ctx", 0, 0, tiled=True, axis_index_groups=groups)

    def small_call(kernel, name, count):
        return pl.pallas_call(kernel, out_shape=struct((count, depth, 128), BF), compiler_params=params(SMALL), name=name)

    total = (part_own + part_got.astype(F32)).astype(BF)
    scattered = swap(total, along)
    scattered, gated_top, mixed_top = lax.optimization_barrier((scattered, gated_top, mixed_top))
    before = shifted(gated_top, 1)
    rim = shifted(mixed_top, -1)
    crossed = swap(small_call(line_kernel, "line", lines)(scattered), across)
    gathered = swap(small_call(piece_kernel, "piece", blocks)(crossed), along)
    grads = run_rest(1, run_rest(0, (), before, rim), before, rim)
    gathered, query_grad, value_grad = lax.optimization_barrier((gathered, *grads))
    ways = lax.axis_size("tp")
    norms = pl.pallas_call(
        norm_kernel,
        out_shape=struct((2 * ways, 1, 128), F32),
        compiler_params=params(SMALL),
        name="norm",
    )(gathered)
    norms = lax.all_to_all(norms, ("tp", "dp"), 0, 0, tiled=True)
    other = lax.ppermute(gathered, "dp", [(0, 1), (1, 0)])
    limit = math.sqrt((long_len + short_len) * chan_width * ways)
    whole = pl.BlockSpec((blocks, depth, 128), lambda i, core: (0, 0, 0))

    def result(rows):
        return pl.BlockSpec((rows, half_width), lambda i, core: (0, jnp.where(i == 0, core[0], 1 - core[0])))

    long_grad, short_grad = pl.pallas_call(
        functools.partial(scale_kernel, limit),
        out_shape=(struct((long_len, chan_width), BF), struct((short_len, chan_width), BF)),
        grid_spec=pltpu.PrefetchScalarGridSpec(
            num_scalar_prefetch=1,
            grid=(2,),
            in_specs=[whole, whole, pl.BlockSpec((2 * ways, 1, 128), lambda i, core: (0, 0, 0))],
            out_specs=[result(long_len), result(short_len)],
        ),
        compiler_params=params(SMALL),
        name="scale",
    )(core, gathered, other, norms)
    return (query_grad[None], key_grad[None], value_grad[None], long_grad, short_grad)


def solution(mesh):
    split = P("dp", "ctx", "tp")
    taps = P(None, "tp")
    return jax.shard_map(
        on_device,
        mesh=mesh,
        in_specs=(split, split, split, split, taps, taps),
        out_specs=(split, split, split, taps, taps),
        check_vma=False,
    )
```

```python
import functools
import math

import jax
import jax.numpy as jnp
import numpy as np
from jax import lax
from jax.experimental import pallas as pl
from jax.experimental.pallas import tpu as pltpu
from jax.sharding import PartitionSpec as P

BF = jnp.bfloat16
F32 = jnp.float32
ROWS = 128
WIDTH = 512
VMEM = 60 * 1024 * 1024
SMALL = 16 * 1024 * 1024


def split_table(table):
    high = table.astype(np.float32).astype(jnp.bfloat16)
    low = (table - high.astype(np.float64)).astype(np.float32).astype(jnp.bfloat16)
    return high, low


def tables():
    freq = np.arange(128)[:, None]
    place = np.arange(256)[None, :]
    angle = (freq * place % 256) * (2.0 * np.pi / 256)
    fwd = np.concatenate([np.cos(angle), -np.sin(angle)], axis=0)
    fwd[128] = 1.0 - 2.0 * (np.arange(256) % 2)
    weight = np.full((256,), 2.0 / 256)
    weight[0] = weight[128] = 1.0 / 256
    inv = (fwd * weight[:, None]).T
    fwd_hi, fwd_lo = split_table(fwd)
    inv_hi, inv_lo = split_table(inv)
    near = np.concatenate([fwd_hi[:, :128], fwd_lo[:, :128]], axis=1)
    away = np.concatenate([fwd_hi[:, 128:], fwd_lo[:, 128:]], axis=1)
    inv_both = np.concatenate([inv_hi[:ROWS], inv_lo[:ROWS]], axis=0)
    return fwd_hi, fwd_lo, near, away, inv_both


def half_of(slot, core):
    return jnp.where(core == 0, 1 - slot, slot)


def by_parity(place_ref, body):
    @pl.when(place_ref[0] >= 2)
    def _():
        body(0, 1)

    @pl.when(place_ref[0] < 2)
    def _():
        body(1, 0)


def gate_kernel(place_ref, query_ref, key_ref, value_ref, grad_ref, taps_ref, first_ref, second_ref, mixed_ref, wide_ref):
    short_len = taps_ref.shape[0]
    width = wide_ref.shape[1]

    def body(up_at, down_at):
        up_ref, down_ref = (first_ref, second_ref)[up_at], (first_ref, second_ref)[down_at]
        down_ref[...] = (grad_ref[...].astype(F32) * query_ref[...].astype(F32)).astype(BF)
        wide_ref[0:8, :] = jnp.zeros((8, width), F32)
        wide_ref[8:, :] = value_ref[...].astype(F32)
        total = taps_ref[0:1, :] * wide_ref[8 : 8 + ROWS, :]
        for lag in range(1, short_len):
            total = total + taps_ref[lag : lag + 1, :] * wide_ref[8 - lag : 8 - lag + ROWS, :]
        mixed = total.astype(BF)
        mixed_ref[...] = mixed
        gated = key_ref[...].astype(F32) * mixed.astype(F32)
        row = lax.broadcasted_iota(jnp.int32, (8, width), 0)
        wide_ref[0:16, :] = gated[0:16]
        top = jnp.where(row < 2, wide_ref[6:14, :], wide_ref[ROWS : ROWS + 8, :])
        up_ref[0:16, :] = jnp.concatenate([top, gated[8:16]], axis=0).astype(BF)
        up_ref[16:ROWS, :] = gated[16:].astype(BF)

    by_parity(place_ref, body)


def own_head(wide_ref, tail, key_ref, value_ref, taps_ref):
    value = value_ref[0:16, :].astype(F32)[0:8]
    key = key_ref[0:16, :].astype(F32)[0:8]
    wide_ref[0:8, :] = tail
    wide_ref[8:16, :] = value
    total = taps_ref[0:1, :] * value
    for lag in range(1, taps_ref.shape[0]):
        total = total + taps_ref[lag : lag + 1, :] * wide_ref[8 - lag : 16 - lag, :]
    mixed = total.astype(BF).astype(F32)
    return mixed, (key * mixed).astype(BF).astype(F32)


def early_rows(wide_ref, got_top):
    row = lax.broadcasted_iota(jnp.int32, got_top.shape, 0)
    wide_ref[8:16, :] = got_top
    return jnp.where(row < 6, 0.0, wide_ref[2:10, :])


def with_heads(own_head_rows, up_ref, got_head_rows, got_ref):
    parts = []
    for head, ref in ((own_head_rows, up_ref), (got_head_rows, got_ref)):
        parts.append(jnp.concatenate([head, ref[0:16, :].astype(F32)[8:16]], axis=0).astype(BF))
        parts.append(ref[16:ROWS, :])
    return jnp.concatenate(parts, axis=0)


def dot(left, right):
    return jnp.dot(left, right, preferred_element_type=F32)


def product(first, second, conjugate):
    first_re, first_im = first[:128], first[128:]
    second_re, second_im = second[:128], second[128:]
    edge = lax.broadcasted_iota(jnp.int32, first_re.shape, 0) == 0
    cross = first_im * second_im
    inner = jnp.where(edge, 0.0, cross)
    if conjugate:
        real = first_re * second_re + inner
        imag = first_im * second_re - first_re * second_im
    else:
        real = first_re * second_re - inner
        imag = first_re * second_im + first_im * second_re
    return jnp.concatenate([real, jnp.where(edge, cross, imag)], axis=0)


def inverse(inv_ref, spec):
    high = spec.astype(BF)
    low = (spec - high.astype(F32)).astype(BF)
    both = dot(inv_ref[...], high)
    return both[:ROWS] + both[ROWS:] + dot(inv_ref[0:ROWS, :], low)


def twice(rows):
    return jnp.concatenate([rows, rows], axis=0)


def sums_kernel(
    place_ref, sent_a_ref, sent_b_ref, got_a_ref, got_b_ref, mixed_ref, key_ref, value_ref, short_ref, long_ref,
    hi_ref, lo_ref, near_ref, away_ref, inv_ref, *rest,
):
    sent, arrived = (sent_a_ref, sent_b_ref), (got_a_ref, got_b_ref)

    def body(up_at, down_at):
        sums_body(
            sent[up_at], arrived[down_at], sent[down_at], arrived[up_at], mixed_ref, key_ref, value_ref, short_ref, long_ref,
            hi_ref, lo_ref, near_ref, away_ref, inv_ref, *rest[-6:],
        )

    by_parity(place_ref, body)


def sums_body(
    up_ref, got_ref, down_ref, back_ref, mixed_ref, key_ref, value_ref, short_ref, long_ref,
    hi_ref, lo_ref, near_ref, away_ref, inv_ref, key_out, mixed_out, gated_top_out, mixed_top_out, part_ref, wide_ref,
):
    short_len = short_ref.shape[0]
    width = wide_ref.shape[1]
    got_top = got_ref[0:16, :].astype(F32)[0:8]
    mixed_top, gated_top = own_head(wide_ref, got_top, key_ref, value_ref, short_ref)
    gated_top_out[...] = gated_top.astype(BF)
    gated = with_heads(gated_top, up_ref, early_rows(wide_ref, got_top), got_ref)
    mid = down_ref[...]
    gated_spec = dot(hi_ref[...], gated) + dot(lo_ref[...], gated)
    mid_spec = dot(near_ref[...], twice(mid))
    both_spec = mid_spec + dot(away_ref[...], twice(back_ref[...]))
    taps_spec = dot(near_ref[...], twice(long_ref[...]))
    long_sum = inverse(inv_ref, product(mid_spec, gated_spec, True))
    gated_grad = inverse(inv_ref, product(both_spec, taps_spec, True))
    next_top = back_ref[0:16, :].astype(F32)[0:8]
    lines = [jnp.zeros((3, width), F32)]
    for gap in range(5, 0, -1):
        line = gated_top[gap : gap + 1] * next_top[0:1]
        for r in range(gap + 1, 6):
            line = line + gated_top[r : r + 1] * next_top[r - gap : r - gap + 1]
        lines.append(line)
    long_end = long_sum[ROWS - 8 :] + jnp.concatenate(lines, axis=0)
    long_sum = jnp.concatenate([long_sum[: ROWS - 8], long_end], axis=0)
    mixed = jnp.concatenate([mixed_top, mixed_ref[0:16, :].astype(F32)[8:16], mixed_ref[16:, :].astype(F32)], axis=0)
    key_out[...] = (gated_grad * mixed).astype(BF)
    mixed_grad = (gated_grad * key_ref[...].astype(F32)).astype(BF)
    mixed_out[...] = mixed_grad
    mixed_grad = mixed_grad.astype(F32)
    mixed_top_out[...] = mixed_grad[0:8].astype(BF)
    wide_ref[0:8, :] = got_top
    wide_ref[8:, :] = value_ref[...].astype(F32)
    sums = []
    for lag in range(short_len):
        sums.append(jnp.sum(mixed_grad * wide_ref[8 - lag : 8 - lag + ROWS, :], axis=0, keepdims=True))
    short_sum = jnp.concatenate(sums + [jnp.zeros((16 - short_len, width), F32)], axis=0)
    for block in range(width // 128):
        lanes = slice(block * 128, block * 128 + 128)
        part_ref[block, 0:ROWS, :] = long_sum[:, lanes].astype(part_ref.dtype)
        part_ref[block, ROWS : ROWS + 16, :] = short_sum[:, lanes].astype(part_ref.dtype)


def rest_kernel(
    place_ref, sent_a_ref, sent_b_ref, got_a_ref, got_b_ref, gated_top_ref, grad_ref, mixed_ref, short_ref, long_ref,
    hi_ref, lo_ref, near_ref, inv_ref, *rest,
):
    query_out, value_out, long_top_out, wide_ref = rest[-4:]
    sent, arrived = (sent_a_ref, sent_b_ref), (got_a_ref, got_b_ref)

    def body(up_at, down_at):
        up_ref, got_ref = sent[up_at], arrived[down_at]
        before = early_rows(wide_ref, got_ref[0:16, :].astype(F32)[0:8])
        gated = with_heads(gated_top_ref[...].astype(F32), up_ref, before, got_ref)
        gated_spec = dot(hi_ref[...], gated) + dot(lo_ref[...], gated)
        taps_spec = dot(near_ref[...], twice(long_ref[...]))
        long_out = inverse(inv_ref, product(gated_spec, taps_spec, False))
        long_top_out[...] = long_out[0:8]
        query_out[...] = (grad_ref[...].astype(F32) * long_out).astype(BF)
        wide_ref[0:ROWS, :] = mixed_ref[...].astype(F32)
        wide_ref[ROWS:, :] = jnp.zeros((8, wide_ref.shape[1]), F32)
        total = short_ref[0:1, :] * wide_ref[0:ROWS, :]
        for lag in range(1, short_ref.shape[0]):
            total = total + short_ref[lag : lag + 1, :] * wide_ref[lag : lag + ROWS, :]
        value_out[...] = total.astype(BF)

    by_parity(place_ref, body)


def edge_kernel(
    before_ref, rim_ref, long_top_ref, grad_ref, taps_ref, mixed_ref, short_ref, query_ref, value_ref,
    query_out, value_out, wide_ref,
):
    width = wide_ref.shape[1]
    before = before_ref[...].astype(F32)
    ends = taps_ref[...].astype(F32)
    lines = []
    for t in range(5):
        line = ends[15:16] * before[t + 1 : t + 2]
        for r in range(t + 2, 6):
            line = line + ends[16 - r + t : 17 - r + t] * before[r : r + 1]
        lines.append(line)
    lines.append(jnp.zeros((3, width), F32))
    long_out = long_top_ref[...] + jnp.concatenate(lines, axis=0)
    query = grad_ref[...].astype(F32)[0:8] * long_out
    query_out[...] = jnp.concatenate([query, query_ref[...].astype(F32)[8:16]], axis=0).astype(BF)
    wide_ref[0:16, :] = mixed_ref[...].astype(F32)
    wide_ref[16:, :] = rim_ref[...].astype(F32)
    total = short_ref[0:1, :] * wide_ref[0:16, :]
    for lag in range(1, short_ref.shape[0]):
        total = total + short_ref[lag : lag + 1, :] * wide_ref[lag : lag + 16, :]
    value_out[...] = total.astype(BF)


def line_kernel(arrived_ref, spread_ref):
    total = arrived_ref[0].astype(F32)
    for device in range(1, arrived_ref.shape[0]):
        total = total + arrived_ref[device].astype(F32)
    message = total.astype(BF)
    for device in range(spread_ref.shape[0]):
        spread_ref[device] = message


def piece_kernel(arrived_ref, spread_ref):
    total = arrived_ref[0].astype(F32)
    for device in range(1, arrived_ref.shape[0]):
        total = total + arrived_ref[device].astype(F32)
    square = jnp.sum(jnp.sum(total * total, axis=1, keepdims=True), axis=0, keepdims=True)
    high = square.astype(BF).astype(F32)
    row = lax.broadcasted_iota(jnp.int32, (8, 128), 0)
    norm_rows = jnp.where(row == 0, high, jnp.where(row == 1, square - high, 0.0))
    message = jnp.concatenate([total[: ROWS + 8], norm_rows], axis=0).astype(BF)
    for device in range(spread_ref.shape[0]):
        spread_ref[device] = message


def norm_kernel(pieces_ref, norm_ref):
    total = pieces_ref[0, ROWS:, :].astype(F32)
    for piece in range(1, pieces_ref.shape[0]):
        total = total + pieces_ref[piece, ROWS:, :].astype(F32)
    square = total[8:9] + total[9:10]
    norm_ref[...] = jnp.broadcast_to(square[None], norm_ref.shape)


def scale_kernel(limit, place_ref, mine_ref, other_ref, norms_ref, long_ref, short_ref):
    norm_sq = norms_ref[0]
    for device in range(1, norms_ref.shape[0]):
        norm_sq = norm_sq + norms_ref[device]
    factor = limit / jnp.sqrt(norm_sq + 1e-06)
    short_len = short_ref.shape[0]

    def write(pieces_ref):
        for block in range(pieces_ref.shape[0]):
            lanes = slice(block * 128, block * 128 + 128)
            piece = pieces_ref[block].astype(F32) * factor
            long_ref[:, lanes] = piece[:ROWS].astype(BF)
            short_ref[:, lanes] = piece[ROWS : ROWS + short_len].astype(BF)

    @pl.when(pl.program_id(0) == 0)
    def _():
        write(mine_ref)

    @pl.when(pl.program_id(0) == 1)
    def _():
        write(other_ref)


def params(limit=VMEM):
    return pltpu.CompilerParams(vmem_limit_bytes=limit)


def swapped(value, phase):
    devices = lax.axis_size("ctx")
    starts = range(1 - phase, devices - 1, 2)
    return lax.ppermute(value, "ctx", [(i, i + 1) for i in starts] + [(i + 1, i) for i in starts])


def shifted(value, by):
    devices = lax.axis_size("ctx")
    return lax.ppermute(value, "ctx", [(i, i + by) for i in range(devices) if 0 <= i + by < devices])


def on_device(gate_query, gate_key, input_value, out_grad, short_taps, long_taps):
    query_rows, key_rows, value_rows, grad_rows = gate_query[0], gate_key[0], input_value[0], out_grad[0]
    chan_width = query_rows.shape[1]
    half_width = chan_width // 2
    short_len, long_len = short_taps.shape[0], long_taps.shape[0]
    core = (lax.axis_index("dp") + 2 * (lax.axis_index("ctx") % 2)).astype(jnp.int32).reshape(1)
    devices = lax.axis_size("ctx")
    per_half = half_width // WIDTH
    struct = jax.ShapeDtypeStruct
    def half(slot):
        return lambda rows: pl.BlockSpec((rows, WIDTH), lambda i, core: (0, half_of(slot, core[0] % 2) * per_half + i))

    def held(rows):
        return pl.BlockSpec((rows, WIDTH), lambda i, core: (0, i))

    def call(kernel, name, slot, operands, specs, kept, out_shape, out_specs, cost):
        first = 1 + len(specs)
        return pl.pallas_call(
            kernel,
            out_shape=out_shape,
            grid_spec=pltpu.PrefetchScalarGridSpec(
                num_scalar_prefetch=1,
                grid=(per_half,),
                in_specs=specs + [pl.BlockSpec(memory_space=pl.ANY)] * len(kept),
                out_specs=out_specs,
                scratch_shapes=[pltpu.VMEM((ROWS + 8, WIDTH), F32)],
            ),
            input_output_aliases={first + k: k for k in range(len(kept))},
            compiler_params=params(),
            cost_estimate=cost,
            name=f"{name}_{slot}",
        )(core, *operands, *kept)

    little = pl.CostEstimate(flops=1000, bytes_accessed=1000, transcendentals=0)
    wide = struct((ROWS, chan_width), BF)
    top = struct((8, chan_width), BF)
    own = struct((ROWS, half_width), BF)
    sent, mixeds, got = [], [], []
    for slot in range(2):
        part = half(slot)
        first, second, mixed = call(
            gate_kernel, "gates", slot, (query_rows, key_rows, value_rows, grad_rows, short_taps),
            [part(ROWS), part(ROWS), part(ROWS), part(ROWS), part(short_len)], (),
            (own, own, own), [held(ROWS)] * 3, little,
        )
        sent.append((first, second))
        mixeds.append(mixed)
        got.append((swapped(first, 0), swapped(second, 1)))
    sent = lax.optimization_barrier(sent)

    fwd_hi, fwd_lo, near, away, inv_both = (jnp.asarray(t) for t in tables())
    table = pl.BlockSpec((256, 256), lambda i, core: (0, 0))

    def run_sums(slot, kept):
        part = half(slot)
        return call(
            sums_kernel, "sums", slot,
            (
                *sent[slot], *got[slot], mixeds[slot], key_rows, value_rows, short_taps, long_taps,
                fwd_hi, fwd_lo, near, away, inv_both,
            ),
            [held(ROWS)] * 5 + [part(ROWS), part(ROWS), part(short_len), part(long_len)] + [table] * 5,
            kept,
            (wide, wide, top, top, struct((half_width // 128, ROWS + 16, 128), BF if slot == 0 else F32)),
            [part(ROWS), part(ROWS), part(8), part(8), pl.BlockSpec((WIDTH // 128, ROWS + 16, 128), lambda i, core: (i, 0, 0))],
            pl.CostEstimate(flops=6_000_000_000, bytes_accessed=8_000_000, transcendentals=0),
        )

    def run_rest(slot, kept):
        part = half(slot)
        return call(
            rest_kernel, "rest", slot,
            (*sent[slot], *got[slot], gated_top, grad_rows, mixed_grad, short_taps, long_taps, fwd_hi, fwd_lo, near, inv_both),
            [held(ROWS)] * 4 + [part(8), part(ROWS), part(ROWS), part(short_len), part(long_len)] + [table] * 4,
            kept,
            (wide, wide, struct((8, chan_width), F32)),
            [part(ROWS), part(ROWS), part(8)],
            pl.CostEstimate(flops=2_000_000_000, bytes_accessed=4_000_000, transcendentals=0),
        )

    *kept, part_sent = run_sums(0, ())
    part_got = lax.ppermute(part_sent, "dp", [(0, 1), (1, 0)])
    key_grad, mixed_grad, gated_top, mixed_top, part_own = run_sums(1, tuple(kept))

    blocks = half_width // 128
    lines = devices // blocks
    along = [[line * blocks + i for i in range(blocks)] for line in range(lines)]
    across = [[line * blocks + i for line in range(lines)] for i in range(blocks)]
    depth = ROWS + 16

    def swap(value, groups):
        return lax.all_to_all(value, "ctx", 0, 0, tiled=True, axis_index_groups=groups)

    def small_call(kernel, name, count):
        return pl.pallas_call(kernel, out_shape=struct((count, depth, 128), BF), compiler_params=params(SMALL), name=name)

    total = (part_own + part_got.astype(F32)).astype(BF)
    scattered = swap(total, along)
    scattered, gated_top, mixed_top, *grads = lax.optimization_barrier((scattered, gated_top, mixed_top, *run_rest(0, ())))
    before = shifted(gated_top, 1)
    rim = shifted(mixed_top, -1)
    crossed = swap(small_call(line_kernel, "line", lines)(scattered), across)
    crossed, *grads = lax.optimization_barrier((crossed, *run_rest(1, tuple(grads))))
    query_grad, value_grad, long_top = grads
    gathered = swap(small_call(piece_kernel, "piece", blocks)(crossed), along)

    def rows_at(rows, index):
        return pl.BlockSpec((rows, chan_width), lambda i: (index, 0))

    last = ROWS // 16 - 1
    query_grad, value_grad = pl.pallas_call(
        edge_kernel,
        out_shape=(wide, wide),
        grid=(1,),
        in_specs=[
            rows_at(8, 0), rows_at(8, 0), rows_at(8, 0), rows_at(16, 0), rows_at(16, long_len // 16 - 1), rows_at(16, last),
            rows_at(short_len, 0), rows_at(16, 0), pl.BlockSpec(memory_space=pl.ANY),
        ],
        out_specs=[rows_at(16, 0), rows_at(16, last)],
        scratch_shapes=[pltpu.VMEM((24, chan_width), F32)],
        input_output_aliases={7: 0, 8: 1},
        compiler_params=params(),
        cost_estimate=pl.CostEstimate(flops=1_000_000, bytes_accessed=500_000, transcendentals=0),
        name="edge",
    )(before, rim, long_top, grad_rows, long_taps, mixed_grad, short_taps, query_grad, value_grad)
    gathered, query_grad, value_grad = lax.optimization_barrier((gathered, query_grad, value_grad))

    ways = lax.axis_size("tp")
    norms = pl.pallas_call(
        norm_kernel,
        out_shape=struct((2 * ways, 1, 128), F32),
        compiler_params=params(SMALL),
        name="norm",
    )(gathered)
    norms = lax.all_to_all(norms, ("tp", "dp"), 0, 0, tiled=True)
    other = lax.ppermute(gathered, "dp", [(0, 1), (1, 0)])
    limit = math.sqrt((long_len + short_len) * chan_width * ways)
    whole = pl.BlockSpec((blocks, depth, 128), lambda i, core: (0, 0, 0))

    def result(rows):
        return pl.BlockSpec((rows, half_width), lambda i, core: (0, jnp.where(i == 0, core[0] % 2, 1 - core[0] % 2)))

    long_grad, short_grad = pl.pallas_call(
        functools.partial(scale_kernel, limit),
        out_shape=(struct((long_len, chan_width), BF), struct((short_len, chan_width), BF)),
        grid_spec=pltpu.PrefetchScalarGridSpec(
            num_scalar_prefetch=1,
            grid=(2,),
            in_specs=[whole, whole, pl.BlockSpec((2 * ways, 1, 128), lambda i, core: (0, 0, 0))],
            out_specs=[result(long_len), result(short_len)],
        ),
        compiler_params=params(SMALL),
        name="scale",
    )(core, gathered, other, norms)
    return (query_grad[None], key_grad[None], value_grad[None], long_grad, short_grad)


def solution(mesh):
    split = P("dp", "ctx", "tp")
    taps = P(None, "tp")
    return jax.shard_map(
        on_device,
        mesh=mesh,
        in_specs=(split, split, split, split, taps, taps),
        out_specs=(split, split, split, taps, taps),
        check_vma=False,
    )
```

```python
import functools
import math

import jax
import jax.numpy as jnp
import numpy as np
from jax import lax
from jax.experimental import pallas as pl
from jax.experimental.pallas import tpu as pltpu
from jax.sharding import PartitionSpec as P

BF = jnp.bfloat16
F32 = jnp.float32
ROWS = 128
WIDTH = 512
VMEM = 60 * 1024 * 1024
SMALL = 16 * 1024 * 1024


def split_table(table):
    high = table.astype(np.float32).astype(jnp.bfloat16)
    low = (table - high.astype(np.float64)).astype(np.float32).astype(jnp.bfloat16)
    return high, low


def tables():
    freq = np.arange(128)[:, None]
    place = np.arange(256)[None, :]
    angle = (freq * place % 256) * (2.0 * np.pi / 256)
    fwd = np.concatenate([np.cos(angle), -np.sin(angle)], axis=0)
    fwd[128] = 1.0 - 2.0 * (np.arange(256) % 2)
    weight = np.full((256,), 2.0 / 256)
    weight[0] = weight[128] = 1.0 / 256
    inv = (fwd * weight[:, None]).T
    fwd_hi, fwd_lo = split_table(fwd)
    inv_hi, inv_lo = split_table(inv)
    near = np.concatenate([fwd_hi[:, :128], fwd_lo[:, :128]], axis=1)
    away = np.concatenate([fwd_hi[:, 128:], fwd_lo[:, 128:]], axis=1)
    inv_both = np.concatenate([inv_hi[:ROWS], inv_lo[:ROWS]], axis=0)
    return fwd_hi, fwd_lo, near, away, inv_both


def half_of(slot, core):
    return jnp.where(core == 0, 1 - slot, slot)


def by_parity(place_ref, body):
    @pl.when(place_ref[0] >= 2)
    def _():
        body(0, 1)

    @pl.when(place_ref[0] < 2)
    def _():
        body(1, 0)


def gate_kernel(place_ref, query_ref, key_ref, value_ref, grad_ref, taps_ref, first_ref, second_ref, mixed_ref, wide_ref):
    short_len = taps_ref.shape[0]
    width = wide_ref.shape[1]

    def body(up_at, down_at):
        up_ref, down_ref = (first_ref, second_ref)[up_at], (first_ref, second_ref)[down_at]
        down_ref[...] = (grad_ref[...].astype(F32) * query_ref[...].astype(F32)).astype(BF)
        wide_ref[0:8, :] = jnp.zeros((8, width), F32)
        wide_ref[8:, :] = value_ref[...].astype(F32)
        total = taps_ref[0:1, :] * wide_ref[8 : 8 + ROWS, :]
        for lag in range(1, short_len):
            total = total + taps_ref[lag : lag + 1, :] * wide_ref[8 - lag : 8 - lag + ROWS, :]
        mixed = total.astype(BF)
        mixed_ref[...] = mixed
        gated = key_ref[...].astype(F32) * mixed.astype(F32)
        row = lax.broadcasted_iota(jnp.int32, (8, width), 0)
        wide_ref[0:16, :] = gated[0:16]
        top = jnp.where(row < 2, wide_ref[6:14, :], wide_ref[ROWS : ROWS + 8, :])
        up_ref[0:16, :] = jnp.concatenate([top, gated[8:16]], axis=0).astype(BF)
        up_ref[16:ROWS, :] = gated[16:].astype(BF)

    by_parity(place_ref, body)


def own_head(wide_ref, tail, key_ref, value_ref, taps_ref):
    value = value_ref[0:16, :].astype(F32)[0:8]
    key = key_ref[0:16, :].astype(F32)[0:8]
    wide_ref[0:8, :] = tail
    wide_ref[8:16, :] = value
    total = taps_ref[0:1, :] * value
    for lag in range(1, taps_ref.shape[0]):
        total = total + taps_ref[lag : lag + 1, :] * wide_ref[8 - lag : 16 - lag, :]
    mixed = total.astype(BF).astype(F32)
    return mixed, (key * mixed).astype(BF).astype(F32)


def early_rows(wide_ref, got_top):
    row = lax.broadcasted_iota(jnp.int32, got_top.shape, 0)
    wide_ref[8:16, :] = got_top
    return jnp.where(row < 6, 0.0, wide_ref[2:10, :])


def with_heads(own_head_rows, up_ref, got_head_rows, got_ref):
    parts = []
    for head, ref in ((own_head_rows, up_ref), (got_head_rows, got_ref)):
        parts.append(jnp.concatenate([head, ref[0:16, :].astype(F32)[8:16]], axis=0).astype(BF))
        parts.append(ref[16:ROWS, :])
    return jnp.concatenate(parts, axis=0)


def dot(left, right):
    return jnp.dot(left, right, preferred_element_type=F32)


def product(first, second, conjugate):
    first_re, first_im = first[:128], first[128:]
    second_re, second_im = second[:128], second[128:]
    edge = lax.broadcasted_iota(jnp.int32, first_re.shape, 0) == 0
    cross = first_im * second_im
    inner = jnp.where(edge, 0.0, cross)
    if conjugate:
        real = first_re * second_re + inner
        imag = first_im * second_re - first_re * second_im
    else:
        real = first_re * second_re - inner
        imag = first_re * second_im + first_im * second_re
    return jnp.concatenate([real, jnp.where(edge, cross, imag)], axis=0)


def inverse(inv_ref, spec):
    high = spec.astype(BF)
    low = (spec - high.astype(F32)).astype(BF)
    both = dot(inv_ref[...], high)
    return both[:ROWS] + both[ROWS:] + dot(inv_ref[0:ROWS, :], low)


def twice(rows):
    return jnp.concatenate([rows, rows], axis=0)


def sums_kernel(
    place_ref, sent_a_ref, sent_b_ref, got_a_ref, got_b_ref, mixed_ref, key_ref, value_ref, short_ref, long_ref,
    hi_ref, lo_ref, near_ref, away_ref, inv_ref, *rest,
):
    key_out, mixed_out, *tops, part_ref, wide_ref = rest[-6:]
    sent, arrived = (sent_a_ref, sent_b_ref), (got_a_ref, got_b_ref)

    def body(up_at, down_at):
        sums_body(
            sent[up_at], arrived[down_at], sent[down_at], arrived[up_at], mixed_ref, key_ref, value_ref, short_ref, long_ref,
            hi_ref, lo_ref, near_ref, away_ref, inv_ref, key_out, mixed_out, tops[up_at], tops[down_at], part_ref, wide_ref,
        )

    by_parity(place_ref, body)


def sums_body(
    up_ref, got_ref, down_ref, back_ref, mixed_ref, key_ref, value_ref, short_ref, long_ref,
    hi_ref, lo_ref, near_ref, away_ref, inv_ref, key_out, mixed_out, gated_top_out, mixed_top_out, part_ref, wide_ref,
):
    short_len = short_ref.shape[0]
    width = wide_ref.shape[1]
    got_top = got_ref[0:16, :].astype(F32)[0:8]
    mixed_top, gated_top = own_head(wide_ref, got_top, key_ref, value_ref, short_ref)
    gated_top_out[...] = gated_top.astype(BF)
    gated = with_heads(gated_top, up_ref, early_rows(wide_ref, got_top), got_ref)
    mid = down_ref[...]
    gated_spec = dot(hi_ref[...], gated) + dot(lo_ref[...], gated)
    mid_spec = dot(near_ref[...], twice(mid))
    both_spec = mid_spec + dot(away_ref[...], twice(back_ref[...]))
    taps_spec = dot(near_ref[...], twice(long_ref[...]))
    long_sum = inverse(inv_ref, product(mid_spec, gated_spec, True))
    gated_grad = inverse(inv_ref, product(both_spec, taps_spec, True))
    next_top = back_ref[0:16, :].astype(F32)[0:8]
    lines = [jnp.zeros((3, width), F32)]
    for gap in range(5, 0, -1):
        line = gated_top[gap : gap + 1] * next_top[0:1]
        for r in range(gap + 1, 6):
            line = line + gated_top[r : r + 1] * next_top[r - gap : r - gap + 1]
        lines.append(line)
    long_end = long_sum[ROWS - 8 :] + jnp.concatenate(lines, axis=0)
    long_sum = jnp.concatenate([long_sum[: ROWS - 8], long_end], axis=0)
    mixed = jnp.concatenate([mixed_top, mixed_ref[0:16, :].astype(F32)[8:16], mixed_ref[16:, :].astype(F32)], axis=0)
    key_out[...] = (gated_grad * mixed).astype(BF)
    mixed_grad = (gated_grad * key_ref[...].astype(F32)).astype(BF)
    mixed_out[...] = mixed_grad
    mixed_grad = mixed_grad.astype(F32)
    mixed_top_out[...] = mixed_grad[0:8].astype(BF)
    wide_ref[0:8, :] = got_top
    wide_ref[8:, :] = value_ref[...].astype(F32)
    sums = []
    for lag in range(short_len):
        sums.append(jnp.sum(mixed_grad * wide_ref[8 - lag : 8 - lag + ROWS, :], axis=0, keepdims=True))
    short_sum = jnp.concatenate(sums + [jnp.zeros((16 - short_len, width), F32)], axis=0)
    for block in range(width // 128):
        lanes = slice(block * 128, block * 128 + 128)
        part_ref[block, 0:ROWS, :] = long_sum[:, lanes].astype(part_ref.dtype)
        part_ref[block, ROWS : ROWS + 16, :] = short_sum[:, lanes].astype(part_ref.dtype)


def rest_kernel(
    place_ref, sent_a_ref, sent_b_ref, got_a_ref, got_b_ref, top_a_ref, top_b_ref, grad_ref, mixed_ref, short_ref, long_ref,
    hi_ref, lo_ref, near_ref, inv_ref, *rest,
):
    query_out, value_out, long_top_out, wide_ref = rest[-4:]
    sent, arrived = (sent_a_ref, sent_b_ref), (got_a_ref, got_b_ref)

    def body(up_at, down_at):
        up_ref, got_ref = sent[up_at], arrived[down_at]
        before = early_rows(wide_ref, got_ref[0:16, :].astype(F32)[0:8])
        gated_top = (top_a_ref, top_b_ref)[up_at][...].astype(F32)
        gated = with_heads(gated_top, up_ref, before, got_ref)
        gated_spec = dot(hi_ref[...], gated) + dot(lo_ref[...], gated)
        taps_spec = dot(near_ref[...], twice(long_ref[...]))
        long_out = inverse(inv_ref, product(gated_spec, taps_spec, False))
        long_top_out[...] = long_out[0:8]
        query_out[...] = (grad_ref[...].astype(F32) * long_out).astype(BF)
        wide_ref[0:ROWS, :] = mixed_ref[...].astype(F32)
        wide_ref[ROWS:, :] = jnp.zeros((8, wide_ref.shape[1]), F32)
        total = short_ref[0:1, :] * wide_ref[0:ROWS, :]
        for lag in range(1, short_ref.shape[0]):
            total = total + short_ref[lag : lag + 1, :] * wide_ref[lag : lag + ROWS, :]
        value_out[...] = total.astype(BF)

    by_parity(place_ref, body)


def edge_kernel(
    place_ref, got_a_ref, got_b_ref, long_top_ref, grad_ref, taps_ref, mixed_ref, short_ref, query_ref, value_ref,
    query_out, value_out, wide_ref,
):
    arrived = (got_a_ref, got_b_ref)

    def body(up_at, down_at):
        before = arrived[down_at][...].astype(F32)
        ends = taps_ref[...].astype(F32)
        lines = []
        for t in range(5):
            line = ends[15:16] * before[t + 1 : t + 2]
            for r in range(t + 2, 6):
                line = line + ends[16 - r + t : 17 - r + t] * before[r : r + 1]
            lines.append(line)
        lines.append(jnp.zeros((3, wide_ref.shape[1]), F32))
        long_out = long_top_ref[...] + jnp.concatenate(lines, axis=0)
        query = grad_ref[...].astype(F32)[0:8] * long_out
        query_out[...] = jnp.concatenate([query, query_ref[...].astype(F32)[8:16]], axis=0).astype(BF)
        wide_ref[0:16, :] = mixed_ref[...].astype(F32)
        wide_ref[16:, :] = arrived[up_at][...].astype(F32)
        total = short_ref[0:1, :] * wide_ref[0:16, :]
        for lag in range(1, short_ref.shape[0]):
            total = total + short_ref[lag : lag + 1, :] * wide_ref[lag : lag + 16, :]
        value_out[...] = total.astype(BF)

    by_parity(place_ref, body)


def line_kernel(arrived_ref, spread_ref):
    total = arrived_ref[0].astype(F32)
    for device in range(1, arrived_ref.shape[0]):
        total = total + arrived_ref[device].astype(F32)
    message = total.astype(BF)
    for device in range(spread_ref.shape[0]):
        spread_ref[device] = message


def piece_kernel(arrived_ref, spread_ref):
    total = arrived_ref[0].astype(F32)
    for device in range(1, arrived_ref.shape[0]):
        total = total + arrived_ref[device].astype(F32)
    square = jnp.sum(jnp.sum(total * total, axis=1, keepdims=True), axis=0, keepdims=True)
    high = square.astype(BF).astype(F32)
    row = lax.broadcasted_iota(jnp.int32, (8, 128), 0)
    norm_rows = jnp.where(row == 0, high, jnp.where(row == 1, square - high, 0.0))
    message = jnp.concatenate([total[: ROWS + 8], norm_rows], axis=0).astype(BF)
    for device in range(spread_ref.shape[0]):
        spread_ref[device] = message


def norm_kernel(pieces_ref, norm_ref):
    total = pieces_ref[0, ROWS:, :].astype(F32)
    for piece in range(1, pieces_ref.shape[0]):
        total = total + pieces_ref[piece, ROWS:, :].astype(F32)
    square = total[8:9] + total[9:10]
    norm_ref[...] = jnp.broadcast_to(square[None], norm_ref.shape)


def scale_kernel(limit, place_ref, mine_ref, other_ref, norms_ref, long_ref, short_ref):
    norm_sq = norms_ref[0]
    for device in range(1, norms_ref.shape[0]):
        norm_sq = norm_sq + norms_ref[device]
    factor = limit / jnp.sqrt(norm_sq + 1e-06)
    short_len = short_ref.shape[0]

    def write(pieces_ref):
        for block in range(pieces_ref.shape[0]):
            lanes = slice(block * 128, block * 128 + 128)
            piece = pieces_ref[block].astype(F32) * factor
            long_ref[:, lanes] = piece[:ROWS].astype(BF)
            short_ref[:, lanes] = piece[ROWS : ROWS + short_len].astype(BF)

    @pl.when(pl.program_id(0) == 0)
    def _():
        write(mine_ref)

    @pl.when(pl.program_id(0) == 1)
    def _():
        write(other_ref)


def params(limit=VMEM):
    return pltpu.CompilerParams(vmem_limit_bytes=limit)


def swapped(value, phase):
    devices = lax.axis_size("ctx")
    starts = range(1 - phase, devices - 1, 2)
    return lax.ppermute(value, "ctx", [(i, i + 1) for i in starts] + [(i + 1, i) for i in starts])


def on_device(gate_query, gate_key, input_value, out_grad, short_taps, long_taps):
    query_rows, key_rows, value_rows, grad_rows = gate_query[0], gate_key[0], input_value[0], out_grad[0]
    chan_width = query_rows.shape[1]
    half_width = chan_width // 2
    short_len, long_len = short_taps.shape[0], long_taps.shape[0]
    core = (lax.axis_index("dp") + 2 * (lax.axis_index("ctx") % 2)).astype(jnp.int32).reshape(1)
    devices = lax.axis_size("ctx")
    per_half = half_width // WIDTH
    struct = jax.ShapeDtypeStruct
    def half(slot):
        return lambda rows: pl.BlockSpec((rows, WIDTH), lambda i, core: (0, half_of(slot, core[0] % 2) * per_half + i))

    def held(rows):
        return pl.BlockSpec((rows, WIDTH), lambda i, core: (0, i))

    def call(kernel, name, slot, operands, specs, kept, out_shape, out_specs, cost):
        first = 1 + len(specs)
        return pl.pallas_call(
            kernel,
            out_shape=out_shape,
            grid_spec=pltpu.PrefetchScalarGridSpec(
                num_scalar_prefetch=1,
                grid=(per_half,),
                in_specs=specs + [pl.BlockSpec(memory_space=pl.ANY)] * len(kept),
                out_specs=out_specs,
                scratch_shapes=[pltpu.VMEM((ROWS + 8, WIDTH), F32)],
            ),
            input_output_aliases={first + k: k for k in range(len(kept))},
            compiler_params=params(),
            cost_estimate=cost,
            name=f"{name}_{slot}",
        )(core, *operands, *kept)

    little = pl.CostEstimate(flops=1000, bytes_accessed=1000, transcendentals=0)
    wide = struct((ROWS, chan_width), BF)
    top = struct((8, chan_width), BF)
    own = struct((ROWS, half_width), BF)
    sent, mixeds, got = [], [], []
    for slot in range(2):
        part = half(slot)
        first, second, mixed = call(
            gate_kernel, "gates", slot, (query_rows, key_rows, value_rows, grad_rows, short_taps),
            [part(ROWS), part(ROWS), part(ROWS), part(ROWS), part(short_len)], (),
            (own, own, own), [held(ROWS)] * 3, little,
        )
        sent.append((first, second))
        mixeds.append(mixed)
        got.append((swapped(first, 0), swapped(second, 1)))
    sent = lax.optimization_barrier(sent)

    fwd_hi, fwd_lo, near, away, inv_both = (jnp.asarray(t) for t in tables())
    table = pl.BlockSpec((256, 256), lambda i, core: (0, 0))

    def run_sums(slot, kept):
        part = half(slot)
        return call(
            sums_kernel, "sums", slot,
            (
                *sent[slot], *got[slot], mixeds[slot], key_rows, value_rows, short_taps, long_taps,
                fwd_hi, fwd_lo, near, away, inv_both,
            ),
            [held(ROWS)] * 5 + [part(ROWS), part(ROWS), part(short_len), part(long_len)] + [table] * 5,
            kept,
            (wide, wide, top, top, struct((half_width // 128, ROWS + 16, 128), BF if slot == 0 else F32)),
            [part(ROWS), part(ROWS), part(8), part(8), pl.BlockSpec((WIDTH // 128, ROWS + 16, 128), lambda i, core: (i, 0, 0))],
            pl.CostEstimate(flops=6_000_000_000, bytes_accessed=8_000_000, transcendentals=0),
        )

    def run_rest(slot, kept):
        part = half(slot)
        return call(
            rest_kernel, "rest", slot,
            (*sent[slot], *got[slot], *tops, grad_rows, mixed_grad, short_taps, long_taps, fwd_hi, fwd_lo, near, inv_both),
            [held(ROWS)] * 4 + [part(8), part(8), part(ROWS), part(ROWS), part(short_len), part(long_len)] + [table] * 4,
            kept,
            (wide, wide, struct((8, chan_width), F32)),
            [part(ROWS), part(ROWS), part(8)],
            pl.CostEstimate(flops=2_000_000_000, bytes_accessed=4_000_000, transcendentals=0),
        )

    *kept, part_sent = run_sums(0, ())
    part_got = lax.ppermute(part_sent, "dp", [(0, 1), (1, 0)])
    key_grad, mixed_grad, *tops, part_own = run_sums(1, tuple(kept))

    blocks = half_width // 128
    lines = devices // blocks
    along = [[line * blocks + i for i in range(blocks)] for line in range(lines)]
    across = [[line * blocks + i for line in range(lines)] for i in range(blocks)]
    depth = ROWS + 16

    def swap(value, groups):
        return lax.all_to_all(value, "ctx", 0, 0, tiled=True, axis_index_groups=groups)

    def small_call(kernel, name, count):
        return pl.pallas_call(kernel, out_shape=struct((count, depth, 128), BF), compiler_params=params(SMALL), name=name)

    total = (part_own + part_got.astype(F32)).astype(BF)
    scattered = swap(total, along)
    got_tops = [swapped(tops[phase], phase) for phase in range(2)]
    scattered, got_tops, *grads = lax.optimization_barrier((scattered, got_tops, *run_rest(0, ())))
    crossed = swap(small_call(line_kernel, "line", lines)(scattered), across)
    crossed, *grads = lax.optimization_barrier((crossed, *run_rest(1, tuple(grads))))
    query_grad, value_grad, long_top = grads
    gathered = swap(small_call(piece_kernel, "piece", blocks)(crossed), along)

    def rows_at(rows, index):
        return pl.BlockSpec((rows, chan_width), lambda i, core: (index, 0))

    last = ROWS // 16 - 1
    query_grad, value_grad = pl.pallas_call(
        edge_kernel,
        out_shape=(wide, wide),
        grid_spec=pltpu.PrefetchScalarGridSpec(
            num_scalar_prefetch=1,
            grid=(1,),
            in_specs=[
                rows_at(8, 0), rows_at(8, 0), rows_at(8, 0), rows_at(16, 0), rows_at(16, long_len // 16 - 1), rows_at(16, last),
                rows_at(short_len, 0), rows_at(16, 0), pl.BlockSpec(memory_space=pl.ANY),
            ],
            out_specs=[rows_at(16, 0), rows_at(16, last)],
            scratch_shapes=[pltpu.VMEM((24, chan_width), F32)],
        ),
        input_output_aliases={8: 0, 9: 1},
        compiler_params=params(),
        cost_estimate=pl.CostEstimate(flops=1_000_000, bytes_accessed=500_000, transcendentals=0),
        name="edge",
    )(core, *got_tops, long_top, grad_rows, long_taps, mixed_grad, short_taps, query_grad, value_grad)
    gathered, query_grad, value_grad = lax.optimization_barrier((gathered, query_grad, value_grad))

    ways = lax.axis_size("tp")
    norms = pl.pallas_call(
        norm_kernel,
        out_shape=struct((2 * ways, 1, 128), F32),
        compiler_params=params(SMALL),
        name="norm",
    )(gathered)
    norms = lax.all_to_all(norms, ("tp", "dp"), 0, 0, tiled=True)
    other = lax.ppermute(gathered, "dp", [(0, 1), (1, 0)])
    limit = math.sqrt((long_len + short_len) * chan_width * ways)
    whole = pl.BlockSpec((blocks, depth, 128), lambda i, core: (0, 0, 0))

    def result(rows):
        return pl.BlockSpec((rows, half_width), lambda i, core: (0, jnp.where(i == 0, core[0] % 2, 1 - core[0] % 2)))

    long_grad, short_grad = pl.pallas_call(
        functools.partial(scale_kernel, limit),
        out_shape=(struct((long_len, chan_width), BF), struct((short_len, chan_width), BF)),
        grid_spec=pltpu.PrefetchScalarGridSpec(
            num_scalar_prefetch=1,
            grid=(2,),
            in_specs=[whole, whole, pl.BlockSpec((2 * ways, 1, 128), lambda i, core: (0, 0, 0))],
            out_specs=[result(long_len), result(short_len)],
        ),
        compiler_params=params(SMALL),
        name="scale",
    )(core, gathered, other, norms)
    return (query_grad[None], key_grad[None], value_grad[None], long_grad, short_grad)


def solution(mesh):
    split = P("dp", "ctx", "tp")
    taps = P(None, "tp")
    return jax.shard_map(
        on_device,
        mesh=mesh,
        in_specs=(split, split, split, split, taps, taps),
        out_specs=(split, split, split, taps, taps),
        check_vma=False,
    )
```

```python
import functools
import math

import jax
import jax.numpy as jnp
import numpy as np
from jax import lax
from jax.experimental import pallas as pl
from jax.experimental.pallas import tpu as pltpu
from jax.sharding import PartitionSpec as P

BF = jnp.bfloat16
F32 = jnp.float32
ROWS = 128
WIDTH = 512
VMEM = 60 * 1024 * 1024
SMALL = 16 * 1024 * 1024


def split_table(table):
    high = table.astype(np.float32).astype(jnp.bfloat16)
    low = (table - high.astype(np.float64)).astype(np.float32).astype(jnp.bfloat16)
    return high, low


def tables():
    freq = np.arange(128)[:, None]
    place = np.arange(256)[None, :]
    angle = (freq * place % 256) * (2.0 * np.pi / 256)
    fwd = np.concatenate([np.cos(angle), -np.sin(angle)], axis=0)
    fwd[128] = 1.0 - 2.0 * (np.arange(256) % 2)
    weight = np.full((256,), 2.0 / 256)
    weight[0] = weight[128] = 1.0 / 256
    inv = (fwd * weight[:, None]).T
    fwd_hi, fwd_lo = split_table(fwd)
    inv_hi, inv_lo = split_table(inv)
    near = np.concatenate([fwd_hi[:, :128], fwd_lo[:, :128]], axis=1)
    away = np.concatenate([fwd_hi[:, 128:], fwd_lo[:, 128:]], axis=1)
    inv_both = np.concatenate([inv_hi[:ROWS], inv_lo[:ROWS]], axis=0)
    return fwd_hi, fwd_lo, near, away, inv_both


def half_of(slot, core):
    return jnp.where(core == 0, 1 - slot, slot)


def by_parity(place_ref, body):
    @pl.when(place_ref[0] >= 2)
    def _():
        body(0, 1)

    @pl.when(place_ref[0] < 2)
    def _():
        body(1, 0)


def gate_kernel(place_ref, query_ref, key_ref, value_ref, grad_ref, taps_ref, first_ref, second_ref, mixed_ref, wide_ref):
    short_len = taps_ref.shape[0]
    width = wide_ref.shape[1]

    def body(up_at, down_at):
        up_ref, down_ref = (first_ref, second_ref)[up_at], (first_ref, second_ref)[down_at]
        down_ref[...] = (grad_ref[...].astype(F32) * query_ref[...].astype(F32)).astype(BF)
        wide_ref[0:8, :] = jnp.zeros((8, width), F32)
        wide_ref[8:, :] = value_ref[...].astype(F32)
        total = taps_ref[0:1, :] * wide_ref[8 : 8 + ROWS, :]
        for lag in range(1, short_len):
            total = total + taps_ref[lag : lag + 1, :] * wide_ref[8 - lag : 8 - lag + ROWS, :]
        mixed = total.astype(BF)
        mixed_ref[...] = mixed
        gated = key_ref[...].astype(F32) * mixed.astype(F32)
        row = lax.broadcasted_iota(jnp.int32, (8, width), 0)
        wide_ref[0:16, :] = gated[0:16]
        top = jnp.where(row < 2, wide_ref[6:14, :], wide_ref[ROWS : ROWS + 8, :])
        up_ref[0:16, :] = jnp.concatenate([top, gated[8:16]], axis=0).astype(BF)
        up_ref[16:ROWS, :] = gated[16:].astype(BF)

    by_parity(place_ref, body)


def own_head(wide_ref, tail, key_ref, value_ref, taps_ref):
    value = value_ref[0:16, :].astype(F32)[0:8]
    key = key_ref[0:16, :].astype(F32)[0:8]
    wide_ref[0:8, :] = tail
    wide_ref[8:16, :] = value
    total = taps_ref[0:1, :] * value
    for lag in range(1, taps_ref.shape[0]):
        total = total + taps_ref[lag : lag + 1, :] * wide_ref[8 - lag : 16 - lag, :]
    mixed = total.astype(BF).astype(F32)
    return mixed, (key * mixed).astype(BF).astype(F32)


def early_rows(wide_ref, got_top):
    row = lax.broadcasted_iota(jnp.int32, got_top.shape, 0)
    wide_ref[8:16, :] = got_top
    return jnp.where(row < 6, 0.0, wide_ref[2:10, :])


def with_heads(own_head_rows, up_ref, got_head_rows, got_ref):
    parts = []
    for head, ref in ((own_head_rows, up_ref), (got_head_rows, got_ref)):
        parts.append(jnp.concatenate([head, ref[0:16, :].astype(F32)[8:16]], axis=0).astype(BF))
        parts.append(ref[16:ROWS, :])
    return jnp.concatenate(parts, axis=0)


def dot(left, right):
    return jnp.dot(left, right, preferred_element_type=F32)


def product(first, second, conjugate):
    first_re, first_im = first[:128], first[128:]
    second_re, second_im = second[:128], second[128:]
    edge = lax.broadcasted_iota(jnp.int32, first_re.shape, 0) == 0
    cross = first_im * second_im
    inner = jnp.where(edge, 0.0, cross)
    if conjugate:
        real = first_re * second_re + inner
        imag = first_im * second_re - first_re * second_im
    else:
        real = first_re * second_re - inner
        imag = first_re * second_im + first_im * second_re
    return jnp.concatenate([real, jnp.where(edge, cross, imag)], axis=0)


def inverse(inv_ref, spec):
    high = spec.astype(BF)
    low = (spec - high.astype(F32)).astype(BF)
    both = dot(inv_ref[...], high)
    return both[:ROWS] + both[ROWS:] + dot(inv_ref[0:ROWS, :], low)


def twice(rows):
    return jnp.concatenate([rows, rows], axis=0)


def sums_kernel(
    place_ref, sent_a_ref, sent_b_ref, got_a_ref, got_b_ref, mixed_ref, key_ref, value_ref, short_ref, long_ref,
    hi_ref, lo_ref, near_ref, away_ref, inv_ref, *rest,
):
    key_out, mixed_out, *tops, part_ref, wide_ref = rest[-6:]
    sent, arrived = (sent_a_ref, sent_b_ref), (got_a_ref, got_b_ref)

    def body(up_at, down_at):
        sums_body(
            sent[up_at], arrived[down_at], sent[down_at], arrived[up_at], mixed_ref, key_ref, value_ref, short_ref, long_ref,
            hi_ref, lo_ref, near_ref, away_ref, inv_ref, key_out, mixed_out, tops[up_at], tops[down_at], part_ref, wide_ref,
        )

    by_parity(place_ref, body)


def sums_body(
    up_ref, got_ref, down_ref, back_ref, mixed_ref, key_ref, value_ref, short_ref, long_ref,
    hi_ref, lo_ref, near_ref, away_ref, inv_ref, key_out, mixed_out, gated_top_out, mixed_top_out, part_ref, wide_ref,
):
    short_len = short_ref.shape[0]
    width = wide_ref.shape[1]
    got_top = got_ref[0:16, :].astype(F32)[0:8]
    mixed_top, gated_top = own_head(wide_ref, got_top, key_ref, value_ref, short_ref)
    gated_top_out[...] = gated_top.astype(BF)
    gated = with_heads(gated_top, up_ref, early_rows(wide_ref, got_top), got_ref)
    mid = down_ref[...]
    gated_spec = dot(hi_ref[...], gated) + dot(lo_ref[...], gated)
    mid_spec = dot(near_ref[...], twice(mid))
    both_spec = mid_spec + dot(away_ref[...], twice(back_ref[...]))
    taps_spec = dot(near_ref[...], twice(long_ref[...]))
    long_sum = inverse(inv_ref, product(mid_spec, gated_spec, True))
    gated_grad = inverse(inv_ref, product(both_spec, taps_spec, True))
    next_top = back_ref[0:16, :].astype(F32)[0:8]
    lines = [jnp.zeros((3, width), F32)]
    for gap in range(5, 0, -1):
        line = gated_top[gap : gap + 1] * next_top[0:1]
        for r in range(gap + 1, 6):
            line = line + gated_top[r : r + 1] * next_top[r - gap : r - gap + 1]
        lines.append(line)
    long_end = long_sum[ROWS - 8 :] + jnp.concatenate(lines, axis=0)
    long_sum = jnp.concatenate([long_sum[: ROWS - 8], long_end], axis=0)
    mixed = jnp.concatenate([mixed_top, mixed_ref[0:16, :].astype(F32)[8:16], mixed_ref[16:, :].astype(F32)], axis=0)
    key_out[...] = (gated_grad * mixed).astype(BF)
    mixed_grad = (gated_grad * key_ref[...].astype(F32)).astype(BF)
    mixed_out[...] = mixed_grad
    mixed_grad = mixed_grad.astype(F32)
    mixed_top_out[...] = mixed_grad[0:8].astype(BF)
    wide_ref[0:8, :] = got_top
    wide_ref[8:, :] = value_ref[...].astype(F32)
    sums = []
    for lag in range(short_len):
        sums.append(jnp.sum(mixed_grad * wide_ref[8 - lag : 8 - lag + ROWS, :], axis=0, keepdims=True))
    short_sum = jnp.concatenate(sums + [jnp.zeros((16 - short_len, width), F32)], axis=0)
    for block in range(width // 128):
        lanes = slice(block * 128, block * 128 + 128)
        part_ref[block, 0:ROWS, :] = long_sum[:, lanes].astype(part_ref.dtype)
        part_ref[block, ROWS : ROWS + 16, :] = short_sum[:, lanes].astype(part_ref.dtype)


def rest_kernel(
    place_ref, sent_a_ref, sent_b_ref, got_a_ref, got_b_ref, top_a_ref, top_b_ref, grad_ref, mixed_ref, short_ref, long_ref,
    hi_ref, lo_ref, near_ref, inv_ref, *rest,
):
    query_out, value_out, long_top_out, wide_ref = rest[-4:]
    sent, arrived = (sent_a_ref, sent_b_ref), (got_a_ref, got_b_ref)

    def body(up_at, down_at):
        up_ref, got_ref = sent[up_at], arrived[down_at]
        before = early_rows(wide_ref, got_ref[0:16, :].astype(F32)[0:8])
        gated_top = (top_a_ref, top_b_ref)[up_at][...].astype(F32)
        gated = with_heads(gated_top, up_ref, before, got_ref)
        gated_spec = dot(hi_ref[...], gated) + dot(lo_ref[...], gated)
        taps_spec = dot(near_ref[...], twice(long_ref[...]))
        long_out = inverse(inv_ref, product(gated_spec, taps_spec, False))
        long_top_out[...] = long_out[0:8]
        query_out[...] = (grad_ref[...].astype(F32) * long_out).astype(BF)
        wide_ref[0:ROWS, :] = mixed_ref[...].astype(F32)
        wide_ref[ROWS:, :] = jnp.zeros((8, wide_ref.shape[1]), F32)
        total = short_ref[0:1, :] * wide_ref[0:ROWS, :]
        for lag in range(1, short_ref.shape[0]):
            total = total + short_ref[lag : lag + 1, :] * wide_ref[lag : lag + ROWS, :]
        value_out[...] = total.astype(BF)

    by_parity(place_ref, body)


def edge_kernel(
    place_ref, got_a_ref, got_b_ref, long_top_ref, grad_ref, taps_ref, mixed_ref, short_ref, query_ref, value_ref,
    query_out, value_out, wide_ref,
):
    arrived = (got_a_ref, got_b_ref)

    def body(up_at, down_at):
        before = arrived[down_at][...].astype(F32)
        ends = taps_ref[...].astype(F32)
        lines = []
        for t in range(5):
            line = ends[15:16] * before[t + 1 : t + 2]
            for r in range(t + 2, 6):
                line = line + ends[16 - r + t : 17 - r + t] * before[r : r + 1]
            lines.append(line)
        lines.append(jnp.zeros((3, wide_ref.shape[1]), F32))
        long_out = long_top_ref[...] + jnp.concatenate(lines, axis=0)
        query = grad_ref[...].astype(F32)[0:8] * long_out
        query_out[...] = jnp.concatenate([query, query_ref[...].astype(F32)[8:16]], axis=0).astype(BF)
        wide_ref[0:16, :] = mixed_ref[...].astype(F32)
        wide_ref[16:, :] = arrived[up_at][...].astype(F32)
        total = short_ref[0:1, :] * wide_ref[0:16, :]
        for lag in range(1, short_ref.shape[0]):
            total = total + short_ref[lag : lag + 1, :] * wide_ref[lag : lag + 16, :]
        value_out[...] = total.astype(BF)

    by_parity(place_ref, body)


def line_kernel(arrived_ref, spread_ref):
    total = arrived_ref[0].astype(F32)
    for device in range(1, arrived_ref.shape[0]):
        total = total + arrived_ref[device].astype(F32)
    message = total.astype(BF)
    for device in range(spread_ref.shape[0]):
        spread_ref[device] = message


def piece_kernel(arrived_ref, spread_ref):
    total = arrived_ref[0].astype(F32)
    for device in range(1, arrived_ref.shape[0]):
        total = total + arrived_ref[device].astype(F32)
    square = jnp.sum(jnp.sum(total * total, axis=1, keepdims=True), axis=0, keepdims=True)
    high = square.astype(BF).astype(F32)
    row = lax.broadcasted_iota(jnp.int32, (8, 128), 0)
    norm_rows = jnp.where(row == 0, high, jnp.where(row == 1, square - high, 0.0))
    message = jnp.concatenate([total[: ROWS + 8], norm_rows], axis=0).astype(BF)
    for device in range(spread_ref.shape[0]):
        spread_ref[device] = message


def norm_kernel(pieces_ref, norm_ref):
    total = pieces_ref[0, ROWS:, :].astype(F32)
    for piece in range(1, pieces_ref.shape[0]):
        total = total + pieces_ref[piece, ROWS:, :].astype(F32)
    square = total[8:9] + total[9:10]
    norm_ref[...] = jnp.broadcast_to(square[None], norm_ref.shape)


def scale_kernel(limit, place_ref, mine_ref, other_ref, norms_ref, long_ref, short_ref):
    norm_sq = norms_ref[0]
    for device in range(1, norms_ref.shape[0]):
        norm_sq = norm_sq + norms_ref[device]
    factor = limit / jnp.sqrt(norm_sq + 1e-06)
    short_len = short_ref.shape[0]

    def write(pieces_ref):
        for block in range(pieces_ref.shape[0]):
            lanes = slice(block * 128, block * 128 + 128)
            piece = pieces_ref[block].astype(F32) * factor
            long_ref[:, lanes] = piece[:ROWS].astype(BF)
            short_ref[:, lanes] = piece[ROWS : ROWS + short_len].astype(BF)

    @pl.when(pl.program_id(0) == 0)
    def _():
        write(mine_ref)

    @pl.when(pl.program_id(0) == 1)
    def _():
        write(other_ref)


def params(limit=VMEM):
    return pltpu.CompilerParams(vmem_limit_bytes=limit)


def swapped(value, phase):
    devices = lax.axis_size("ctx")
    starts = range(1 - phase, devices - 1, 2)
    return lax.ppermute(value, "ctx", [(i, i + 1) for i in starts] + [(i + 1, i) for i in starts])


def on_device(gate_query, gate_key, input_value, out_grad, short_taps, long_taps):
    query_rows, key_rows, value_rows, grad_rows = gate_query[0], gate_key[0], input_value[0], out_grad[0]
    chan_width = query_rows.shape[1]
    half_width = chan_width // 2
    short_len, long_len = short_taps.shape[0], long_taps.shape[0]
    core = (lax.axis_index("dp") + 2 * (lax.axis_index("ctx") % 2)).astype(jnp.int32).reshape(1)
    devices = lax.axis_size("ctx")
    per_half = half_width // WIDTH
    struct = jax.ShapeDtypeStruct
    def half(slot):
        return lambda rows: pl.BlockSpec((rows, WIDTH), lambda i, core: (0, half_of(slot, core[0] % 2) * per_half + i))

    def held(rows):
        return pl.BlockSpec((rows, WIDTH), lambda i, core: (0, i))

    def call(kernel, name, slot, operands, specs, kept, out_shape, out_specs, cost):
        first = 1 + len(specs)
        return pl.pallas_call(
            kernel,
            out_shape=out_shape,
            grid_spec=pltpu.PrefetchScalarGridSpec(
                num_scalar_prefetch=1,
                grid=(per_half,),
                in_specs=specs + [pl.BlockSpec(memory_space=pl.ANY)] * len(kept),
                out_specs=out_specs,
                scratch_shapes=[pltpu.VMEM((ROWS + 8, WIDTH), F32)],
            ),
            input_output_aliases={first + k: k for k in range(len(kept))},
            compiler_params=params(),
            cost_estimate=cost,
            name=f"{name}_{slot}",
        )(core, *operands, *kept)

    little = pl.CostEstimate(flops=1000, bytes_accessed=1000, transcendentals=0)
    wide = struct((ROWS, chan_width), BF)
    top = struct((8, chan_width), BF)
    own = struct((ROWS, half_width), BF)
    sent, mixeds, got = [], [], []
    for slot in range(2):
        part = half(slot)
        first, second, mixed = call(
            gate_kernel, "gates", slot, (query_rows, key_rows, value_rows, grad_rows, short_taps),
            [part(ROWS), part(ROWS), part(ROWS), part(ROWS), part(short_len)], (),
            (own, own, own), [held(ROWS)] * 3, little,
        )
        sent.append((first, second))
        mixeds.append(mixed)
        got.append((swapped(first, 0), swapped(second, 1)))
    sent = lax.optimization_barrier(sent)

    fwd_hi, fwd_lo, near, away, inv_both = (jnp.asarray(t) for t in tables())
    table = pl.BlockSpec((256, 256), lambda i, core: (0, 0))

    def run_sums(slot, kept):
        part = half(slot)
        return call(
            sums_kernel, "sums", slot,
            (
                *sent[slot], *got[slot], mixeds[slot], key_rows, value_rows, short_taps, long_taps,
                fwd_hi, fwd_lo, near, away, inv_both,
            ),
            [held(ROWS)] * 5 + [part(ROWS), part(ROWS), part(short_len), part(long_len)] + [table] * 5,
            kept,
            (wide, wide, top, top, struct((half_width // 128, ROWS + 16, 128), BF)),
            [part(ROWS), part(ROWS), part(8), part(8), pl.BlockSpec((WIDTH // 128, ROWS + 16, 128), lambda i, core: (i, 0, 0))],
            pl.CostEstimate(flops=6_000_000_000, bytes_accessed=8_000_000, transcendentals=0),
        )

    def run_rest(slot, kept):
        part = half(slot)
        return call(
            rest_kernel, "rest", slot,
            (*sent[slot], *got[slot], *tops, grad_rows, mixed_grad, short_taps, long_taps, fwd_hi, fwd_lo, near, inv_both),
            [held(ROWS)] * 4 + [part(8), part(8), part(ROWS), part(ROWS), part(short_len), part(long_len)] + [table] * 4,
            kept,
            (wide, wide, struct((8, chan_width), F32)),
            [part(ROWS), part(ROWS), part(8)],
            pl.CostEstimate(flops=2_000_000_000, bytes_accessed=4_000_000, transcendentals=0),
        )

    *kept, part_sent = run_sums(0, ())
    part_got = lax.ppermute(part_sent, "dp", [(0, 1), (1, 0)])
    key_grad, mixed_grad, *tops, part_own = run_sums(1, tuple(kept))

    blocks = half_width // 128
    lines = devices // blocks
    along = [[line * blocks + i for i in range(blocks)] for line in range(lines)]
    across = [[line * blocks + i for line in range(lines)] for i in range(blocks)]
    depth = ROWS + 16

    def swap(value, groups):
        return lax.all_to_all(value, "ctx", 0, 0, tiled=True, axis_index_groups=groups)

    def small_call(kernel, name, count):
        return pl.pallas_call(kernel, out_shape=struct((count, depth, 128), BF), compiler_params=params(SMALL), name=name)

    total = (part_own.astype(F32) + part_got.astype(F32)).astype(BF)
    scattered = swap(total, along)
    got_tops = [swapped(tops[phase], phase) for phase in range(2)]
    scattered, got_tops, sent = lax.optimization_barrier((scattered, got_tops, sent))
    crossed = swap(small_call(line_kernel, "line", lines)(scattered), across)
    crossed, *grads = lax.optimization_barrier((crossed, *run_rest(0, ())))
    query_grad, value_grad, long_top = run_rest(1, tuple(grads))
    gathered = swap(small_call(piece_kernel, "piece", blocks)(crossed), along)
    gathered, query_grad, value_grad, long_top = lax.optimization_barrier((gathered, query_grad, value_grad, long_top))

    def rows_at(rows, index):
        return pl.BlockSpec((rows, chan_width), lambda i, core: (index, 0))

    last = ROWS // 16 - 1
    query_grad, value_grad = pl.pallas_call(
        edge_kernel,
        out_shape=(wide, wide),
        grid_spec=pltpu.PrefetchScalarGridSpec(
            num_scalar_prefetch=1,
            grid=(1,),
            in_specs=[
                rows_at(8, 0), rows_at(8, 0), rows_at(8, 0), rows_at(16, 0), rows_at(16, long_len // 16 - 1), rows_at(16, last),
                rows_at(short_len, 0), rows_at(16, 0), pl.BlockSpec(memory_space=pl.ANY),
            ],
            out_specs=[rows_at(16, 0), rows_at(16, last)],
            scratch_shapes=[pltpu.VMEM((24, chan_width), F32)],
        ),
        input_output_aliases={8: 0, 9: 1},
        compiler_params=params(),
        cost_estimate=pl.CostEstimate(flops=4_000_000_000, bytes_accessed=8_000_000, transcendentals=0),
        name="edge",
    )(core, *got_tops, long_top, grad_rows, long_taps, mixed_grad, short_taps, query_grad, value_grad)
    ways = lax.axis_size("tp")
    norms = pl.pallas_call(
        norm_kernel,
        out_shape=struct((2 * ways, 1, 128), F32),
        compiler_params=params(SMALL),
        name="norm",
    )(gathered)
    norms, gathered = lax.optimization_barrier((norms, gathered))
    norms = lax.all_to_all(norms, ("tp", "dp"), 0, 0, tiled=True)
    other = lax.ppermute(gathered, "dp", [(0, 1), (1, 0)])
    limit = math.sqrt((long_len + short_len) * chan_width * ways)
    whole = pl.BlockSpec((blocks, depth, 128), lambda i, core: (0, 0, 0))

    def result(rows):
        return pl.BlockSpec((rows, half_width), lambda i, core: (0, jnp.where(i == 0, core[0] % 2, 1 - core[0] % 2)))

    long_grad, short_grad = pl.pallas_call(
        functools.partial(scale_kernel, limit),
        out_shape=(struct((long_len, chan_width), BF), struct((short_len, chan_width), BF)),
        grid_spec=pltpu.PrefetchScalarGridSpec(
            num_scalar_prefetch=1,
            grid=(2,),
            in_specs=[whole, whole, pl.BlockSpec((2 * ways, 1, 128), lambda i, core: (0, 0, 0))],
            out_specs=[result(long_len), result(short_len)],
        ),
        compiler_params=params(SMALL),
        name="scale",
    )(core, gathered, other, norms)
    return (query_grad[None], key_grad[None], value_grad[None], long_grad, short_grad)


def solution(mesh):
    split = P("dp", "ctx", "tp")
    taps = P(None, "tp")
    return jax.shard_map(
        on_device,
        mesh=mesh,
        in_specs=(split, split, split, split, taps, taps),
        out_specs=(split, split, split, taps, taps),
        check_vma=False,
    )
```
